256 devices in a mesh: stream: 8 (over x, z_lo), tm: 32 (over z_hi, y, core).
Axes of the slice: x: 4, y: 4, z: 8 (z_hi: 4, z_lo: 2; z = z_hi * 2 + z_lo), core: 2. Of those that a mesh axis runs over, the one named last changes fastest.
Arguments:
- latents: bfloat16 [128, 64, 1024], P('stream'), may hold values from -6 to 6
- cache_prev: bfloat16 [128, 8, 1024], P('stream', None, 'tm'), may hold values from -6 to 6
- prev_slot: int32 [128], P('stream'), may hold values from 0 to 127, each once
- lengths: int32 [128], P('stream'), may hold values from 1 to 64, as said below
- conv_in_w: bfloat16 [7, 1024, 1536], P(None, None, 'tm'), may hold values from -0.0625 to 0.0625
- upsample_w: bfloat16 [16, 1536, 768], P(None, None, 'tm'), may hold values from -0.109375 to 0.109375
- alpha_coarse: float32 [1536], P('tm'), may hold values from 0.3 to 3
- alpha_in: float32 [768], replicated, may hold values from 0.3 to 3
- alpha_mid: float32 [768], replicated, may hold values from 0.3 to 3
- dilated_w: bfloat16 [7, 768, 768], P(None, 'tm'), may hold values from -0.078125 to 0.078125
- project_w: bfloat16 [768, 768], replicated, may hold values from -0.21875 to 0.21875
Outputs:
- decoded: bfloat16 [128, 512, 768], P('stream', 'tm')
The draws below stay inside these ranges and needn't reach their ends.
Inputs may be any that keep to these rules, and one draw needn't show every extreme that they name: `prev_slot`: a permutation: every row of cache_prev belongs to exactly one stream. `lengths`: some stream runs through the whole window.
All inputs are finite; a program needn't handle non-finite values.
Results may differ from the reference program's by a relative error of at most 0.0085.
Values may be sent and summed in bfloat16 or wider, within the bound.
No kernel may reach another device: no remote copies, remote signals or barrier semaphores. Data moves between devices by JAX's collectives and lax.ppermute only.
A program may use at most 128 MiB of HBM per device.

```python
import math
import jax
import jax.numpy as jnp
from jax import lax

D = 1024
C1 = 1536
C2 = 768
K = 7
STRIDE = 8
LAT = 64
PAST = 8
STREAMS = 128
FRAMES = 512


def draw_lengths(key, part):
    key = jax.random.fold_in(key, 11)
    values = jax.random.randint(key, (STREAMS,), 1, LAT + 1)
    return values.at[0].set(LAT).astype(jnp.int32)


def levels(rng, extent, pieces, smallest, largest):
    factor_of, own = 1.0, jax.random.fold_in(rng, 6)
    for axis_at, shards_of in pieces:
        heights = jnp.exp(jax.random.uniform(jax.random.fold_in(own, axis_at), (shards_of,), jnp.float32, smallest / len(pieces), largest / len(pieces)))
        factor_of = factor_of * jnp.repeat(heights, extent[axis_at] // shards_of).reshape([-1 if axis == axis_at else 1 for axis in range(len(extent))])
    return factor_of


def gaussian(rng, extent, scale, most, shards=(), kind=jnp.bfloat16):
    drawn = jax.random.normal(rng, extent, jnp.float32) * scale
    if len(shards) > 0:
        drawn = levels(rng, extent, shards, -0.22, 0.18) * drawn
    return jnp.clip(drawn, min=-most, max=most).astype(kind)


def setup_inputs(seed: int = 0) -> dict:
    streams_of = jax.random.split(jax.random.key(seed), 12)
    return {
        "latents": gaussian(streams_of[0], (STREAMS, LAT, D), 1.0, 6.0, ((0, 8),)),
        "cache_prev": gaussian(streams_of[1], (STREAMS, PAST, D), 1.0, 6.0, ((0, 8), (2, 32))),
        "prev_slot": jax.random.permutation(streams_of[2], STREAMS).astype(jnp.int32),
        "lengths": draw_lengths(jax.random.fold_in(streams_of[11], 71), 0),
        "conv_in_w": gaussian(streams_of[4], (K, D, C1), (K * D) ** -0.5, 0.0625, ((2, 32),)),
        "upsample_w": gaussian(streams_of[5], (2 * STRIDE, C1, C2), (2 * C1) ** -0.5, 0.109375, ((2, 32),)),
        "alpha_coarse": jnp.clip(jnp.exp(math.log(3.0) - 2.3025851 * jax.random.uniform(streams_of[6], (C1,), jnp.float32) ** levels(streams_of[6], (C1,), ((0, 32),), -0.2, 0.2)), 0.3, 3.0),
        "alpha_in": jnp.clip(jnp.exp(jax.random.uniform(streams_of[7], (C2,), jnp.float32, math.log(0.3), math.log(3.0))), 0.3, 3.0),
        "alpha_mid": jnp.clip(jnp.exp(jax.random.uniform(streams_of[8], (C2,), jnp.float32, math.log(0.3), math.log(3.0))), 0.3, 3.0),
        "dilated_w": gaussian(streams_of[9], (K, C2, C2), (K * C2) ** -0.5, 0.078125, ((1, 32),)),
        "project_w": gaussian(streams_of[10], (C2, C2), C2 ** -0.5, 0.21875),
    }


def snake(values, alpha):
    return values + jnp.sin(alpha * values) ** 2 / alpha


def reference(latents, cache_prev, prev_slot, lengths, conv_in_w, upsample_w, alpha_coarse, alpha_in, alpha_mid, dilated_w, project_w):
    history = jnp.take(cache_prev, prev_slot, axis=0)
    extended = jnp.concatenate([history, latents], axis=1)
    stacked_w = jnp.concatenate([upsample_w[:STRIDE], upsample_w[STRIDE:]], axis=1).astype(jnp.float32)

    def one_stream(inputs):
        frames_in, live = inputs
        coarse_sum = jnp.zeros((LAT + 2, C1), jnp.float32)
        for offset in range(K):
            coarse_sum = coarse_sum + jnp.dot(frames_in[offset:offset + LAT + 2], conv_in_w[offset], preferred_element_type=jnp.float32)
        coarse = snake(coarse_sum, alpha_coarse).astype(jnp.bfloat16)
        paired = jnp.concatenate([coarse[1:], coarse[:-1]], axis=1).astype(jnp.float32)
        fine = jnp.einsum("tc,jco->tjo", paired, stacked_w).reshape(STRIDE * (LAT + 1), C2).astype(jnp.bfloat16)
        window = snake(fine[STRIDE - (K - 1):].astype(jnp.float32), alpha_in).astype(jnp.bfloat16)
        response = jnp.zeros((FRAMES, C2), jnp.float32)
        for offset in range(K):
            response = response + jnp.dot(window[offset:offset + FRAMES], dilated_w[offset], preferred_element_type=jnp.float32)
        middle = snake(response, alpha_mid).astype(jnp.bfloat16)
        projected = jnp.dot(middle, project_w, preferred_element_type=jnp.float32)
        summed = fine[STRIDE:].astype(jnp.float32) + projected
        keep = jnp.arange(FRAMES, dtype=jnp.int32) < STRIDE * live
        return jnp.where(keep[:, None], summed, jnp.float32(0.0)).astype(jnp.bfloat16)

    return lax.map(one_stream, (extended, lengths))
```

```python
import functools

import jax
import jax.numpy as jnp
from jax import lax
from jax.experimental import pallas as pl
from jax.experimental.pallas import tpu as pltpu
from jax.sharding import PartitionSpec as P

F32 = jnp.float32
BF16 = jnp.bfloat16
VMEM_LIMIT = 48 * 1024 * 1024


def sin_squared(u):
    k = jnp.floor(u * 0.3183098861837907 + 0.5)
    r = u - k * 3.140625
    r = r - k * 0.0009670257568359375
    r = r - k * 6.2771141529083252e-07
    r = jnp.clip(r, -1.5708, 1.5708)
    q = r * r
    p = -2.5052108385441720e-08
    p = p * q + 2.7557319223985893e-06
    p = p * q - 1.9841269841269841e-04
    p = p * q + 8.3333333333333333e-03
    p = p * q - 1.6666666666666667e-01
    s = r + r * (q * p)
    return s * s


def snake(x, alpha, inverse):
    return x + sin_squared(alpha * x) * inverse


def fill_taps(w_ref, wc_ref):
    taps, _, width = w_ref.shape
    wc_ref[...] = jnp.zeros_like(wc_ref)
    for k in range(taps):
        at = 64 * k
        wc_ref[:, at : at + width] = w_ref[k]


def tap_sum(y, shift, width):
    rows = y.shape[0]
    total = None
    for g in range(y.shape[1] // 128):
        part = y[:, 128 * g : 128 * g + 128]
        turn = (-(2 * g + shift)) % rows
        if turn:
            part = pltpu.roll(part, turn, 0)
        total = part if total is None else total + part
    odd = pltpu.roll(pltpu.roll(total, rows - 1, 0), 64, 1)
    return total + odd


def coarse_kernel(order_ref, lat_ref, w_ref, a_ref, ia_ref, out_ref, wc_ref, v_ref):
    half, frames, depth = lat_ref.shape
    width = out_ref.shape[1]

    @pl.when(pl.program_id(0) == 0)
    def _():
        fill_taps(w_ref, wc_ref)

    x = lat_ref[...].reshape(half * frames, depth)
    y = jnp.dot(x, wc_ref[...], preferred_element_type=F32)
    for s in range(half):
        v_ref[s * frames : (s + 1) * frames, :] = tap_sum(
            y[s * frames : (s + 1) * frames], -6, width
        )
    u = [v_ref[pl.ds(t, half, stride=frames), :] for t in range(frames)]
    u = jnp.concatenate(u, axis=0)
    u = snake(u, a_ref[...], ia_ref[...])
    out_ref[0] = u.T[:width].astype(BF16)


def history_kernel(h_ref, lat_ref, w_ref, a_ref, ia_ref, out_ref, wc_ref, v_ref):
    streams, frames, depth = lat_ref.shape
    width = out_ref.shape[1]
    past = h_ref.shape[1] // streams
    half = streams // 2
    fill_taps(w_ref, wc_ref)
    wc = wc_ref[...]
    ht = h_ref[...].astype(F32).T.astype(BF16)
    yh = jnp.dot(ht, wc, preferred_element_type=F32)
    yl = jnp.dot(
        lat_ref[...].reshape(streams * frames, depth), wc, preferred_element_type=F32
    )
    for s in range(streams):
        z = jnp.concatenate(
            [yh[past * s : past * (s + 1)], yl[frames * s : frames * s + past]], axis=0
        )
        v_ref[past * s : past * (s + 1), :] = tap_sum(z, 0, width)[:past]
    for c in range(2):
        rows = [
            v_ref[pl.ds(c * half * past + i, half, stride=past), :] for i in range(past)
        ]
        gap = jnp.zeros((128 - past * half, 128), F32)
        u = jnp.concatenate(rows[2:] + [gap] + rows[:2], axis=0)
        u = snake(u, a_ref[...], ia_ref[...])
        out_ref[c] = u.T[:width].astype(BF16)


def upsample_kernel(off_ref, x0, x1, x2, x3, xh_ref, w_ref, out_ref, xs_ref, fs_ref):
    width = 48
    n = x0.shape[1]
    pieces = x0.shape[0] // width
    for dy, ref in enumerate((x0, x1, x2, x3)):
        for i in range(pieces):
            at = pl.multiple_of(off_ref[dy * pieces + i], 16)
            xs_ref[pl.ds(at, width), :] = ref[i * width : (i + 1) * width, :]
    rows = w_ref.shape[0]
    half = rows // 2
    r = jnp.dot(w_ref[...], xs_ref[...], preferred_element_type=F32)
    rh = jnp.dot(w_ref[...], xh_ref[...], preferred_element_type=F32)
    lane = lax.broadcasted_iota(jnp.int32, (rows, 128), 1)
    first = jnp.where(lane < 48, rh, r[:, :128])
    r = jnp.concatenate([first, r[:, 128:]], axis=1)
    turned = pltpu.roll(rh[half:], 8, 1)
    shifted = pltpu.roll(r[half:], 8, 1)
    lane = lax.broadcasted_iota(jnp.int32, (half, 128), 1)
    shifted = jnp.concatenate(
        [jnp.where(lane < 8, turned, shifted[:, :128]), shifted[:, 128:]], axis=1
    )
    fs_ref[8 : 8 + n, :] = (r[:half] + shifted).T
    fs_ref[0:8, :] = (rh[:half] + turned).T[120:128]
    blocks, take, _ = out_ref.shape
    for b in range(blocks):
        out_ref[b] = fs_ref[16 * b : 16 * b + take, :].astype(BF16)


def residual_kernel(
    arr_ref, lim_ref, ai_ref, iai_ref, am_ref, iam_ref, wd_ref, wp_ref,
    out_ref, f_ref, win_ref, acc_ref, r_ref,
):
    k = pl.program_id(0)
    taps = pl.num_programs(0)
    rows, channels = acc_ref.shape
    streams = out_ref.shape[0]
    sources, take, _ = arr_ref.shape
    piece = 48
    half = streams // 2

    @pl.when(k == 0)
    def _():
        for c in range(2):
            for j in range(8):
                x = jnp.concatenate(
                    [
                        arr_ref[m, :, piece * j : piece * (j + 1)].astype(F32)
                        for m in range(c, sources, 2)
                    ],
                    axis=1,
                )
                for t in range(take // half):
                    at = (8 * t + j) * streams + half * c
                    f_ref[at : at + half, :] = x[half * t : half * (t + 1)]
        win_ref[...] = snake(f_ref[...], ai_ref[...], iai_ref[...]).astype(BF16)
        acc_ref[...] = jnp.zeros_like(acc_ref)

    at = pl.multiple_of((k + 2) * streams, 16)
    acc_ref[...] += jnp.dot(
        win_ref[pl.ds(at, rows), :], wd_ref[0], preferred_element_type=F32
    )

    @pl.when(k == taps - 1)
    def _():
        middle = snake(acc_ref[...], am_ref[...], iam_ref[...]).astype(BF16)
        summed = f_ref[8 * streams :, :] + jnp.dot(
            middle, wp_ref[...], preferred_element_type=F32
        )
        local = lax.broadcasted_iota(jnp.int32, (rows, channels), 0) // streams
        kept = jnp.where(local < lim_ref[...], summed, 0.0)
        for g in range(channels // 128):
            r_ref[g] = kept[:, 128 * g : 128 * (g + 1)]
        for s in range(streams):
            out_ref[s] = jnp.concatenate(
                [
                    r_ref[g, pl.ds(s, rows // streams, stride=streams), :]
                    for g in range(channels // 128)
                ],
                axis=1,
            ).astype(BF16)


def whole(*shape):
    return pl.BlockSpec(shape, lambda *_: (0,) * len(shape))


def per_device(
    latents,
    cache_prev,
    prev_slot,
    lengths,
    conv_in_w,
    upsample_w,
    alpha_coarse,
    alpha_in,
    alpha_mid,
    dilated_w,
    project_w,
):
    groups, frames, depth = latents.shape
    taps, _, width = conv_in_w.shape
    past = cache_prev.shape[1]
    slab = cache_prev.shape[2]
    half = groups // 2
    channels = dilated_w.shape[2]
    tm = lax.axis_index("tm")
    z, y, core = tm // 8, (tm // 2) % 4, tm % 2

    def turned(dz, dy, flip=0):
        pairs = []
        for m in range(32):
            a, b, c = m // 8, (m // 2) % 4, m % 2
            pairs.append((m, ((a + dz) % 4) * 8 + ((b + dy) % 4) * 2 + (c + flip) % 2))
        return pairs

    def send(x, dz, dy, flip=0):
        return lax.ppermute(x, "tm", turned(dz, dy, flip))

    dilated = lax.all_gather(dilated_w, "tm", axis=1, tiled=True)
    up_t = jnp.transpose(upsample_w, (0, 2, 1))
    up_other = send(up_t, 0, 0, 1)
    up = jnp.where(
        core == 0,
        jnp.concatenate([up_t, up_other], axis=1),
        jnp.concatenate([up_other, up_t], axis=1),
    ).reshape(-1, up_t.shape[2])

    flat = cache_prev.reshape(groups, past * slab)
    every = lax.all_to_all(
        jnp.broadcast_to(flat[None], (8,) + flat.shape), "stream", 0, 0, tiled=True
    ).reshape(8 * groups, past * slab)
    selected = jnp.take(every, prev_slot, axis=0).reshape(groups * past, slab).T
    history = lax.all_to_all(
        jnp.broadcast_to(selected[None], (32,) + selected.shape), "tm", 0, 0, tiled=True
    ).reshape(32 * slab, groups * past)

    pad = 128 - width
    alpha_c = jnp.pad(alpha_coarse, (0, pad), constant_values=1.0)[None]
    inverse_c = 1.0 / alpha_c
    order = jnp.stack([core, 1 - core]).astype(jnp.int32)
    main = pl.pallas_call(
        coarse_kernel,
        grid_spec=pltpu.PrefetchScalarGridSpec(
            num_scalar_prefetch=1,
            grid=(2,),
            in_specs=[
                pl.BlockSpec((half, frames, depth), lambda i, o: (o[i], 0, 0)),
                whole(taps, depth, width),
                whole(1, 128),
                whole(1, 128),
            ],
            out_specs=pl.BlockSpec((1, width, half * frames), lambda i, o: (i, 0, 0)),
            scratch_shapes=[
                pltpu.VMEM((depth, 512), BF16),
                pltpu.VMEM((half * frames, 128), F32),
            ],
        ),
        out_shape=jax.ShapeDtypeStruct((2, width, half * frames), BF16),
        compiler_params=pltpu.CompilerParams(vmem_limit_bytes=VMEM_LIMIT),
        name="coarse_main",
    )(order, latents, conv_in_w, alpha_c, inverse_c)
    own = jnp.concatenate([main[0], send(main[1], 0, 0, 1)], axis=0)
    column = jnp.concatenate([own, send(own, 1, 0), send(own, 2, 0), send(own, 3, 0)], axis=0)
    columns = [column, send(column, 0, 1), send(column, 0, 2), send(column, 0, 3)]

    head = pl.pallas_call(
        history_kernel,
        grid=(1,),
        in_specs=[
            whole(depth, groups * past),
            whole(groups, 16, depth),
            whole(taps, depth, width),
            whole(1, 128),
            whole(1, 128),
        ],
        out_specs=whole(2, width, 128),
        out_shape=jax.ShapeDtypeStruct((2, width, 128), BF16),
        scratch_shapes=[pltpu.VMEM((depth, 512), BF16), pltpu.VMEM((groups * past, 128), F32)],
        compiler_params=pltpu.CompilerParams(vmem_limit_bytes=VMEM_LIMIT),
        name="coarse_history",
    )(history, latents, conv_in_w, alpha_c, inverse_c)
    heads = lax.all_to_all(
        jnp.tile(head, (16, 1, 1)), "tm", 0, 0, tiled=True
    ).reshape(32 * width, 128)

    offsets = []
    for dy in range(4):
        for dz in range(4):
            for flip in range(2):
                source = ((z - dz) % 4) * 8 + ((y - dy) % 4) * 2 + (core + flip) % 2
                offsets.append(source * width)
    offsets = jnp.stack(offsets).astype(jnp.int32)
    n = half * frames
    blocks = pl.pallas_call(
        upsample_kernel,
        grid_spec=pltpu.PrefetchScalarGridSpec(
            num_scalar_prefetch=1,
            grid=(1,),
            in_specs=[whole(8 * width, n)] * 4
            + [whole(32 * width, 128), whole(16 * width, 32 * width)],
            out_specs=whole(32, 24, 8 * width),
            scratch_shapes=[
                pltpu.VMEM((32 * width, n), BF16),
                pltpu.VMEM((n + 8, 8 * width), F32),
            ],
        ),
        out_shape=jax.ShapeDtypeStruct((32, 24, 8 * width), BF16),
        compiler_params=pltpu.CompilerParams(vmem_limit_bytes=VMEM_LIMIT),
        name="upsample",
    )(offsets, *columns, heads, up)
    arrived = lax.all_to_all(blocks, "tm", 0, 0, tiled=True)

    shard = 16
    rows = shard * groups
    limit = 8 * lengths - tm * shard
    limit = jnp.tile(limit, shard)[:, None].astype(jnp.int32)
    return pl.pallas_call(
        residual_kernel,
        grid=(taps,),
        in_specs=[
            whole(32, 24, 8 * width),
            whole(rows, 1),
            whole(1, channels),
            whole(1, channels),
            whole(1, channels),
            whole(1, channels),
            pl.BlockSpec((1, channels, channels), lambda k: (k, 0, 0)),
            whole(channels, channels),
        ],
        out_specs=whole(groups, shard, channels),
        out_shape=jax.ShapeDtypeStruct((groups, shard, channels), BF16),
        scratch_shapes=[
            pltpu.VMEM((24 * groups, channels), F32),
            pltpu.VMEM((24 * groups, channels), BF16),
            pltpu.VMEM((rows, channels), F32),
            pltpu.VMEM((channels // 128, rows, 128), F32),
        ],
        compiler_params=pltpu.CompilerParams(vmem_limit_bytes=VMEM_LIMIT),
        name="residual",
    )(
        arrived,
        limit,
        alpha_in[None],
        (1.0 / alpha_in)[None],
        alpha_mid[None],
        (1.0 / alpha_mid)[None],
        dilated,
        project_w,
    )


def solution(mesh):
    return jax.shard_map(
        per_device,
        mesh=mesh,
        in_specs=(
            P("stream", None, None),
            P("stream", None, "tm"),
            P("stream"),
            P("stream"),
            P(None, None, "tm"),
            P(None, None, "tm"),
            P("tm"),
            P(),
            P(),
            P(None, "tm", None),
            P(),
        ),
        out_specs=P("stream", "tm", None),
        check_vma=False,
    )
```

```python
import functools

import jax
import jax.numpy as jnp
from jax import lax
from jax.experimental import pallas as pl
from jax.experimental.pallas import tpu as pltpu
from jax.sharding import PartitionSpec as P

F32 = jnp.float32
BF16 = jnp.bfloat16
VMEM_LIMIT = 48 * 1024 * 1024


def sin_squared(u):
    k = jnp.floor(u * 0.3183098861837907 + 0.5)
    r = u - k * 3.140625
    r = r - k * 0.0009670257568359375
    r = r - k * 6.2771141529083252e-07
    r = jnp.clip(r, -1.5708, 1.5708)
    q = r * r
    p = -2.5052108385441720e-08
    p = p * q + 2.7557319223985893e-06
    p = p * q - 1.9841269841269841e-04
    p = p * q + 8.3333333333333333e-03
    p = p * q - 1.6666666666666667e-01
    s = r + r * (q * p)
    return s * s


def snake(x, alpha, inverse):
    return x + sin_squared(alpha * x) * inverse


def fill_taps(w_ref, wc_ref):
    taps, _, width = w_ref.shape
    wc_ref[...] = jnp.zeros_like(wc_ref)
    for k in range(taps):
        at = 64 * k
        wc_ref[:, at : at + width] = w_ref[k]


def tap_sum(y, shift, width):
    rows = y.shape[0]
    total = None
    for g in range(y.shape[1] // 128):
        part = y[:, 128 * g : 128 * g + 128]
        turn = (-(2 * g + shift)) % rows
        if turn:
            part = pltpu.roll(part, turn, 0)
        total = part if total is None else total + part
    odd = pltpu.roll(pltpu.roll(total, rows - 1, 0), 64, 1)
    return total + odd


def coarse_kernel(order_ref, lat_ref, w_ref, a_ref, ia_ref, out_ref, wc_ref, v_ref):
    half, frames, depth = lat_ref.shape
    width = out_ref.shape[1]

    @pl.when(pl.program_id(0) == 0)
    def _():
        fill_taps(w_ref, wc_ref)

    x = lat_ref[...].reshape(half * frames, depth)
    y = jnp.dot(x, wc_ref[...], preferred_element_type=F32)
    for s in range(half):
        v_ref[s * frames : (s + 1) * frames, :] = tap_sum(
            y[s * frames : (s + 1) * frames], -6, width
        )
    u = [v_ref[pl.ds(t, half, stride=frames), :] for t in range(frames)]
    u = jnp.concatenate(u, axis=0)
    u = snake(u, a_ref[...], ia_ref[...])
    out_ref[0] = u.T[:width].astype(BF16)


def cached_kernel(h_ref, w_ref, out_ref, wc_ref, v_ref):
    fill_taps(w_ref, wc_ref)
    rows = h_ref.shape[1]
    past = 8
    ht = h_ref[...].astype(F32).T.astype(BF16)
    y = jnp.dot(ht, wc_ref[...], preferred_element_type=F32)
    blank = jnp.zeros((past, y.shape[1]), F32)
    for s in range(rows // past):
        z = jnp.concatenate([y[past * s : past * (s + 1)], blank], axis=0)
        v_ref[past * s : past * (s + 1), :] = tap_sum(z, 0, 48)[:past]
    out_ref[...] = v_ref[...].astype(BF16)


def history_kernel(
    slot_ref, c_ref, lat_ref, w_ref, a_ref, ia_ref, out_ref, wc_ref, v_ref, all_ref
):
    streams, frames, depth = lat_ref.shape
    width = out_ref.shape[1]
    half = streams // 2
    past = 8
    fill_taps(w_ref, wc_ref)
    y = jnp.dot(
        lat_ref[...].reshape(streams * frames, depth),
        wc_ref[...],
        preferred_element_type=F32,
    )
    all_ref[...] = c_ref[...].astype(F32)
    blank = jnp.zeros((past, y.shape[1]), F32)
    for s in range(streams):
        z = jnp.concatenate([blank, y[frames * s : frames * s + past]], axis=0)
        at = pl.multiple_of(slot_ref[s] * past, past)
        cached = all_ref[pl.ds(at, past), :]
        v_ref[past * s : past * (s + 1), :] = tap_sum(z, 0, width)[:past] + cached
    for c in range(2):
        rows = [
            v_ref[pl.ds(c * half * past + i, half, stride=past), :] for i in range(past)
        ]
        gap = jnp.zeros((128 - past * half, 128), F32)
        u = jnp.concatenate(rows[2:] + [gap] + rows[:2], axis=0)
        u = snake(u, a_ref[...], ia_ref[...])
        out_ref[c] = u.T[:width].astype(BF16)


def upsample_kernel(off_ref, *refs):
    x_refs, (xh_ref, w_ref, out_ref, xs_ref, fs_ref) = refs[:8], refs[8:]
    width = 48
    n = xs_ref.shape[1]
    pieces = x_refs[0].shape[0] // width
    for part, ref in enumerate(x_refs):
        for i in range(pieces):
            at = pl.multiple_of(off_ref[part * pieces + i], 16)
            xs_ref[pl.ds(at, width), :] = ref[i * width : (i + 1) * width, :]
    rows = w_ref.shape[0]
    half = rows // 2
    r = jnp.dot(w_ref[...], xs_ref[...], preferred_element_type=F32)
    rh = jnp.dot(w_ref[...], xh_ref[...], preferred_element_type=F32)
    lane = lax.broadcasted_iota(jnp.int32, (rows, 128), 1)
    first = jnp.where(lane < 48, rh, r[:, :128])
    r = jnp.concatenate([first, r[:, 128:]], axis=1)
    turned = pltpu.roll(rh[half:], 8, 1)
    shifted = pltpu.roll(r[half:], 8, 1)
    lane = lax.broadcasted_iota(jnp.int32, (half, 128), 1)
    shifted = jnp.concatenate(
        [jnp.where(lane < 8, turned, shifted[:, :128]), shifted[:, 128:]], axis=1
    )
    fs_ref[8 : 8 + n, :] = (r[:half] + shifted).T
    fs_ref[0:8, :] = (rh[:half] + turned).T[120:128]
    blocks, take, _ = out_ref.shape
    for b in range(blocks):
        out_ref[b] = fs_ref[16 * b : 16 * b + take, :].astype(BF16)


def residual_kernel(
    arr_ref, lim_ref, ai_ref, iai_ref, am_ref, iam_ref, wd_ref, wp_ref,
    out_ref, f_ref, win_ref, acc_ref, r_ref,
):
    k = pl.program_id(0)
    taps = pl.num_programs(0)
    rows, channels = acc_ref.shape
    streams = out_ref.shape[0]
    sources, take, _ = arr_ref.shape
    piece = 48
    half = streams // 2

    @pl.when(k == 0)
    def _():
        for c in range(2):
            for j in range(8):
                x = jnp.concatenate(
                    [
                        arr_ref[m, :, piece * j : piece * (j + 1)].astype(F32)
                        for m in range(c, sources, 2)
                    ],
                    axis=1,
                )
                for t in range(take // half):
                    at = (8 * t + j) * streams + half * c
                    f_ref[at : at + half, :] = x[half * t : half * (t + 1)]
        win_ref[...] = snake(f_ref[...], ai_ref[...], iai_ref[...]).astype(BF16)
        acc_ref[...] = jnp.zeros_like(acc_ref)

    at = pl.multiple_of((k + 2) * streams, 16)
    acc_ref[...] += jnp.dot(
        win_ref[pl.ds(at, rows), :], wd_ref[0], preferred_element_type=F32
    )

    @pl.when(k == taps - 1)
    def _():
        middle = snake(acc_ref[...], am_ref[...], iam_ref[...]).astype(BF16)
        summed = f_ref[8 * streams :, :] + jnp.dot(
            middle, wp_ref[...], preferred_element_type=F32
        )
        local = lax.broadcasted_iota(jnp.int32, (rows, channels), 0) // streams
        kept = jnp.where(local < lim_ref[...], summed, 0.0)
        for g in range(channels // 128):
            r_ref[g] = kept[:, 128 * g : 128 * (g + 1)]
        for s in range(streams):
            out_ref[s] = jnp.concatenate(
                [
                    r_ref[g, pl.ds(s, rows // streams, stride=streams), :]
                    for g in range(channels // 128)
                ],
                axis=1,
            ).astype(BF16)


def after(x, *others):
    return lax.optimization_barrier((x,) + others)[0]


def whole(*shape):
    return pl.BlockSpec(shape, lambda *_: (0,) * len(shape))


def per_device(
    latents,
    cache_prev,
    prev_slot,
    lengths,
    conv_in_w,
    upsample_w,
    alpha_coarse,
    alpha_in,
    alpha_mid,
    dilated_w,
    project_w,
):
    groups, frames, depth = latents.shape
    taps, _, width = conv_in_w.shape
    past = cache_prev.shape[1]
    slab = cache_prev.shape[2]
    half = groups // 2
    channels = dilated_w.shape[2]
    tm = lax.axis_index("tm")
    z, y, core = tm // 8, (tm // 2) % 4, tm % 2

    def turned(dz, dy, flip=0):
        pairs = []
        for m in range(32):
            a, b, c = m // 8, (m // 2) % 4, m % 2
            pairs.append((m, ((a + dz) % 4) * 8 + ((b + dy) % 4) * 2 + (c + flip) % 2))
        return pairs

    def send(x, dz, dy, flip=0):
        return lax.ppermute(x, "tm", turned(dz, dy, flip))

    dilated = lax.all_gather(dilated_w, "tm", axis=1, tiled=True)
    up_t = jnp.transpose(upsample_w, (0, 2, 1))
    up_other = send(up_t, 0, 0, 1)
    up = jnp.where(
        core == 0,
        jnp.concatenate([up_t, up_other], axis=1),
        jnp.concatenate([up_other, up_t], axis=1),
    ).reshape(-1, up_t.shape[2])

    flat = jnp.transpose(cache_prev, (2, 0, 1)).reshape(slab, groups * past)
    cached = lax.all_to_all(
        jnp.broadcast_to(flat[None], (32,) + flat.shape), "tm", 0, 0, tiled=True
    ).reshape(32 * slab, groups * past)
    pad = 128 - width
    alpha_c = jnp.pad(alpha_coarse, (0, pad), constant_values=1.0)[None]
    inverse_c = 1.0 / alpha_c
    order = jnp.stack([core, 1 - core]).astype(jnp.int32)
    main = pl.pallas_call(
        coarse_kernel,
        grid_spec=pltpu.PrefetchScalarGridSpec(
            num_scalar_prefetch=1,
            grid=(2,),
            in_specs=[
                pl.BlockSpec((half, frames, depth), lambda i, o: (o[i], 0, 0)),
                whole(taps, depth, width),
                whole(1, 128),
                whole(1, 128),
            ],
            out_specs=pl.BlockSpec((1, width, half * frames), lambda i, o: (i, 0, 0)),
            scratch_shapes=[
                pltpu.VMEM((depth, 512), BF16),
                pltpu.VMEM((half * frames, 128), F32),
            ],
        ),
        out_shape=jax.ShapeDtypeStruct((2, width, half * frames), BF16),
        compiler_params=pltpu.CompilerParams(vmem_limit_bytes=VMEM_LIMIT),
        name="coarse_main",
    )(order, latents, conv_in_w, alpha_c, inverse_c)
    own = jnp.concatenate([main[0], send(main[1], 0, 0, 1)], axis=0)
    cached = after(cached, own)
    added = pl.pallas_call(
        cached_kernel,
        grid=(1,),
        in_specs=[whole(depth, groups * past), whole(taps, depth, width)],
        out_specs=whole(groups * past, 128),
        out_shape=jax.ShapeDtypeStruct((groups * past, 128), BF16),
        scratch_shapes=[pltpu.VMEM((depth, 512), BF16), pltpu.VMEM((groups * past, 128), F32)],
        compiler_params=pltpu.CompilerParams(vmem_limit_bytes=VMEM_LIMIT),
        name="cached",
    )(cached, conv_in_w)
    every = lax.all_to_all(
        jnp.broadcast_to(added[None], (8,) + added.shape), "stream", 0, 0, tiled=True
    ).reshape(8 * groups * past, 128)
    low = jnp.concatenate([own, send(own, 1, 0)], axis=0)
    high = jnp.concatenate([send(own, 2, 0), send(own, 3, 0)], axis=0)
    up_low, down_low = send(low, 0, 1), send(low, 0, 3)
    up_high, down_high = send(high, 0, 1), send(high, 0, 3)
    far_low, far_high = send(up_low, 0, 1), send(down_high, 0, 3)
    columns = [low, high, up_low, up_high, far_low, far_high, down_low, down_high]

    head = pl.pallas_call(
        history_kernel,
        grid_spec=pltpu.PrefetchScalarGridSpec(
            num_scalar_prefetch=1,
            grid=(1,),
            in_specs=[
                whole(8 * groups * past, 128),
                whole(groups, 16, depth),
                whole(taps, depth, width),
                whole(1, 128),
                whole(1, 128),
            ],
            out_specs=whole(2, width, 128),
            scratch_shapes=[
                pltpu.VMEM((depth, 512), BF16),
                pltpu.VMEM((groups * past, 128), F32),
                pltpu.VMEM((8 * groups * past, 128), F32),
            ],
        ),
        out_shape=jax.ShapeDtypeStruct((2, width, 128), BF16),
        compiler_params=pltpu.CompilerParams(vmem_limit_bytes=VMEM_LIMIT),
        name="coarse_history",
    )(prev_slot, every, latents, conv_in_w, alpha_c, inverse_c)
    heads = lax.all_to_all(
        jnp.tile(head, (16, 1, 1)), "tm", 0, 0, tiled=True
    ).reshape(32 * width, 128)

    offsets = []
    for dy in range(4):
        for dz in range(4):
            for flip in range(2):
                source = ((z - dz) % 4) * 8 + ((y - dy) % 4) * 2 + (core + flip) % 2
                offsets.append(source * width)
    offsets = jnp.stack(offsets).astype(jnp.int32)
    n = half * frames
    blocks = pl.pallas_call(
        upsample_kernel,
        grid_spec=pltpu.PrefetchScalarGridSpec(
            num_scalar_prefetch=1,
            grid=(1,),
            in_specs=[whole(4 * width, n)] * 8
            + [whole(32 * width, 128), whole(16 * width, 32 * width)],
            out_specs=whole(32, 24, 8 * width),
            scratch_shapes=[
                pltpu.VMEM((32 * width, n), BF16),
                pltpu.VMEM((n + 8, 8 * width), F32),
            ],
        ),
        out_shape=jax.ShapeDtypeStruct((32, 24, 8 * width), BF16),
        compiler_params=pltpu.CompilerParams(vmem_limit_bytes=60 * 1024 * 1024),
        name="upsample",
    )(offsets, *columns, heads, up)
    arrived = lax.all_to_all(blocks, "tm", 0, 0, tiled=True)

    shard = 16
    rows = shard * groups
    limit = 8 * lengths - tm * shard
    limit = jnp.tile(limit, shard)[:, None].astype(jnp.int32)
    return pl.pallas_call(
        residual_kernel,
        grid=(taps,),
        in_specs=[
            whole(32, 24, 8 * width),
            whole(rows, 1),
            whole(1, channels),
            whole(1, channels),
            whole(1, channels),
            whole(1, channels),
            pl.BlockSpec((1, channels, channels), lambda k: (k, 0, 0)),
            whole(channels, channels),
        ],
        out_specs=whole(groups, shard, channels),
        out_shape=jax.ShapeDtypeStruct((groups, shard, channels), BF16),
        scratch_shapes=[
            pltpu.VMEM((24 * groups, channels), F32),
            pltpu.VMEM((24 * groups, channels), BF16),
            pltpu.VMEM((rows, channels), F32),
            pltpu.VMEM((channels // 128, rows, 128), F32),
        ],
        compiler_params=pltpu.CompilerParams(vmem_limit_bytes=VMEM_LIMIT),
        name="residual",
    )(
        arrived,
        limit,
        alpha_in[None],
        (1.0 / alpha_in)[None],
        alpha_mid[None],
        (1.0 / alpha_mid)[None],
        dilated,
        project_w,
    )


def solution(mesh):
    return jax.shard_map(
        per_device,
        mesh=mesh,
        in_specs=(
            P("stream", None, None),
            P("stream", None, "tm"),
            P("stream"),
            P("stream"),
            P(None, None, "tm"),
            P(None, None, "tm"),
            P("tm"),
            P(),
            P(),
            P(None, "tm", None),
            P(),
        ),
        out_specs=P("stream", "tm", None),
        check_vma=False,
    )
```

```python
import functools

import jax
import jax.numpy as jnp
from jax import lax
from jax.experimental import pallas as pl
from jax.experimental.pallas import tpu as pltpu
from jax.sharding import PartitionSpec as P

F32 = jnp.float32
BF16 = jnp.bfloat16
VMEM_LIMIT = 48 * 1024 * 1024


def sin_squared(u):
    k = jnp.floor(u * 0.3183098861837907 + 0.5)
    r = u - k * 3.140625
    r = r - k * 0.0009670257568359375
    r = r - k * 6.2771141529083252e-07
    r = jnp.clip(r, -1.5708, 1.5708)
    q = r * r
    p = -2.5052108385441720e-08
    p = p * q + 2.7557319223985893e-06
    p = p * q - 1.9841269841269841e-04
    p = p * q + 8.3333333333333333e-03
    p = p * q - 1.6666666666666667e-01
    s = r + r * (q * p)
    return s * s


def snake(x, alpha, inverse):
    return x + sin_squared(alpha * x) * inverse


def fill_taps(w_ref, wc_ref):
    taps, _, width = w_ref.shape
    wc_ref[...] = jnp.zeros_like(wc_ref)
    for k in range(taps):
        at = 64 * k
        wc_ref[:, at : at + width] = w_ref[k]


def tap_sum(y, shift, width):
    rows = y.shape[0]
    total = None
    for g in range(y.shape[1] // 128):
        part = y[:, 128 * g : 128 * g + 128]
        turn = (-(2 * g + shift)) % rows
        if turn:
            part = pltpu.roll(part, turn, 0)
        total = part if total is None else total + part
    odd = pltpu.roll(pltpu.roll(total, rows - 1, 0), 64, 1)
    return total + odd


def coarse_kernel(order_ref, lat_ref, w_ref, a_ref, ia_ref, out_ref, wc_ref, v_ref):
    half, frames, depth = lat_ref.shape
    width = out_ref.shape[1]

    @pl.when(pl.program_id(0) == 0)
    def _():
        fill_taps(w_ref, wc_ref)

    x = lat_ref[...].reshape(half * frames, depth)
    y = jnp.dot(x, wc_ref[...], preferred_element_type=F32)
    for s in range(half):
        v_ref[s * frames : (s + 1) * frames, :] = tap_sum(
            y[s * frames : (s + 1) * frames], -6, width
        )
    u = [v_ref[pl.ds(t, half, stride=frames), :] for t in range(frames)]
    u = jnp.concatenate(u, axis=0)
    u = snake(u, a_ref[...], ia_ref[...])
    out_ref[0] = u.T[:width].astype(BF16)


def cached_kernel(h_ref, w_ref, out_ref, wc_ref, v_ref):
    fill_taps(w_ref, wc_ref)
    rows = h_ref.shape[1]
    past = 8
    ht = h_ref[...].astype(F32).T.astype(BF16)
    y = jnp.dot(ht, wc_ref[...], preferred_element_type=F32)
    blank = jnp.zeros((past, y.shape[1]), F32)
    for s in range(rows // past):
        z = jnp.concatenate([y[past * s : past * (s + 1)], blank], axis=0)
        v_ref[past * s : past * (s + 1), :] = tap_sum(z, 0, 48)[:past]
    out_ref[...] = v_ref[...].astype(BF16)


def history_kernel(
    slot_ref, c_ref, lat_ref, w_ref, a_ref, ia_ref, out_ref, wc_ref, v_ref, all_ref
):
    streams, frames, depth = lat_ref.shape
    width = out_ref.shape[1]
    half = streams // 2
    past = 8
    fill_taps(w_ref, wc_ref)
    y = jnp.dot(
        lat_ref[...].reshape(streams * frames, depth),
        wc_ref[...],
        preferred_element_type=F32,
    )
    all_ref[...] = c_ref[...].astype(F32)
    blank = jnp.zeros((past, y.shape[1]), F32)
    for s in range(streams):
        z = jnp.concatenate([blank, y[frames * s : frames * s + past]], axis=0)
        at = pl.multiple_of(slot_ref[s] * past, past)
        cached = all_ref[pl.ds(at, past), :]
        v_ref[past * s : past * (s + 1), :] = tap_sum(z, 0, width)[:past] + cached
    for c in range(2):
        rows = [
            v_ref[pl.ds(c * half * past + i, half, stride=past), :] for i in range(past)
        ]
        gap = jnp.zeros((128 - past * half, 128), F32)
        u = jnp.concatenate(rows[2:] + [gap] + rows[:2], axis=0)
        u = snake(u, a_ref[...], ia_ref[...])
        out_ref[c] = u.T[:width].astype(BF16)


def upsample_kernel(off_ref, *refs):
    x_refs, (xh_ref, w_ref, out_ref, xs_ref, fs_ref) = refs[:8], refs[8:]
    width = 48
    n = xs_ref.shape[1]
    pieces = x_refs[0].shape[0] // width
    for part, ref in enumerate(x_refs):
        for i in range(pieces):
            at = pl.multiple_of(off_ref[part * pieces + i], 16)
            xs_ref[pl.ds(at, width), :] = ref[i * width : (i + 1) * width, :]
    rows = w_ref.shape[0]
    half = rows // 2
    r = jnp.dot(w_ref[...], xs_ref[...], preferred_element_type=F32)
    rh = jnp.dot(w_ref[...], xh_ref[...], preferred_element_type=F32)
    lane = lax.broadcasted_iota(jnp.int32, (rows, 128), 1)
    first = jnp.where(lane < 48, rh, r[:, :128])
    r = jnp.concatenate([first, r[:, 128:]], axis=1)
    turned = pltpu.roll(rh[half:], 8, 1)
    shifted = pltpu.roll(r[half:], 8, 1)
    lane = lax.broadcasted_iota(jnp.int32, (half, 128), 1)
    shifted = jnp.concatenate(
        [jnp.where(lane < 8, turned, shifted[:, :128]), shifted[:, 128:]], axis=1
    )
    fs_ref[8 : 8 + n, :] = (r[:half] + shifted).T
    fs_ref[0:8, :] = (rh[:half] + turned).T[120:128]
    blocks, take, _ = out_ref.shape
    for b in range(blocks):
        out_ref[b] = fs_ref[16 * b : 16 * b + take, :].astype(BF16)


def residual_kernel(
    arr_ref, lim_ref, ai_ref, iai_ref, am_ref, iam_ref, wd_hbm, wp_ref,
    out_ref, f_ref, win_ref, r_ref, wd_ref, sems,
):
    streams, shard, channels = out_ref.shape
    rows = streams * shard
    sources, take, _ = arr_ref.shape
    taps = wd_ref.shape[0]
    piece = 48
    half = streams // 2
    copies = [
        pltpu.make_async_copy(wd_hbm.at[k], wd_ref.at[k], sems.at[k])
        for k in range(taps)
    ]
    for copy in copies:
        copy.start()
    for c in range(2):
        for j in range(8):
            x = jnp.concatenate(
                [
                    arr_ref[m, :, piece * j : piece * (j + 1)].astype(F32)
                    for m in range(c, sources, 2)
                ],
                axis=1,
            )
            for t in range(take // half):
                at = (8 * t + j) * streams + half * c
                f_ref[at : at + half, :] = x[half * t : half * (t + 1)]
    used = 2 * streams
    win_ref[used:, :] = snake(f_ref[used:, :], ai_ref[...], iai_ref[...]).astype(BF16)
    total = None
    for k in range(taps):
        copies[k].wait()
        at = (k + 2) * streams
        part = jnp.dot(
            win_ref[at : at + rows, :], wd_ref[k], preferred_element_type=F32
        )
        total = part if total is None else total + part
    middle = snake(total, am_ref[...], iam_ref[...]).astype(BF16)
    summed = f_ref[8 * streams :, :] + jnp.dot(
        middle, wp_ref[...], preferred_element_type=F32
    )
    local = lax.broadcasted_iota(jnp.int32, (rows, channels), 0) // streams
    kept = jnp.where(local < lim_ref[...], summed, 0.0)
    for g in range(channels // 128):
        r_ref[g] = kept[:, 128 * g : 128 * (g + 1)]
    for s in range(streams):
        out_ref[s] = jnp.concatenate(
            [
                r_ref[g, pl.ds(s, shard, stride=streams), :]
                for g in range(channels // 128)
            ],
            axis=1,
        ).astype(BF16)


def after(x, *others):
    return lax.optimization_barrier((x,) + others)[0]


def whole(*shape):
    return pl.BlockSpec(shape, lambda *_: (0,) * len(shape))


def per_device(
    latents,
    cache_prev,
    prev_slot,
    lengths,
    conv_in_w,
    upsample_w,
    alpha_coarse,
    alpha_in,
    alpha_mid,
    dilated_w,
    project_w,
):
    groups, frames, depth = latents.shape
    taps, _, width = conv_in_w.shape
    past = cache_prev.shape[1]
    slab = cache_prev.shape[2]
    half = groups // 2
    channels = dilated_w.shape[2]
    tm = lax.axis_index("tm")
    z, y, core = tm // 8, (tm // 2) % 4, tm % 2

    def turned(dz, dy, flip=0):
        pairs = []
        for m in range(32):
            a, b, c = m // 8, (m // 2) % 4, m % 2
            pairs.append((m, ((a + dz) % 4) * 8 + ((b + dy) % 4) * 2 + (c + flip) % 2))
        return pairs

    def send(x, dz, dy, flip=0):
        return lax.ppermute(x, "tm", turned(dz, dy, flip))

    dilated = lax.all_gather(dilated_w, "tm", axis=1, tiled=True)
    up_t = jnp.transpose(upsample_w, (0, 2, 1))
    up_other = send(up_t, 0, 0, 1)
    up = jnp.where(
        core == 0,
        jnp.concatenate([up_t, up_other], axis=1),
        jnp.concatenate([up_other, up_t], axis=1),
    ).reshape(-1, up_t.shape[2])

    flat = jnp.transpose(cache_prev, (2, 0, 1)).reshape(slab, groups * past)
    cached = lax.all_to_all(
        jnp.broadcast_to(flat[None], (32,) + flat.shape), "tm", 0, 0, tiled=True
    ).reshape(32 * slab, groups * past)
    pad = 128 - width
    alpha_c = jnp.pad(alpha_coarse, (0, pad), constant_values=1.0)[None]
    inverse_c = 1.0 / alpha_c
    order = jnp.stack([core, 1 - core]).astype(jnp.int32)
    main = pl.pallas_call(
        coarse_kernel,
        grid_spec=pltpu.PrefetchScalarGridSpec(
            num_scalar_prefetch=1,
            grid=(2,),
            in_specs=[
                pl.BlockSpec((half, frames, depth), lambda i, o: (o[i], 0, 0)),
                whole(taps, depth, width),
                whole(1, 128),
                whole(1, 128),
            ],
            out_specs=pl.BlockSpec((1, width, half * frames), lambda i, o: (i, 0, 0)),
            scratch_shapes=[
                pltpu.VMEM((depth, 512), BF16),
                pltpu.VMEM((half * frames, 128), F32),
            ],
        ),
        out_shape=jax.ShapeDtypeStruct((2, width, half * frames), BF16),
        compiler_params=pltpu.CompilerParams(vmem_limit_bytes=VMEM_LIMIT),
        name="coarse_main",
    )(order, latents, conv_in_w, alpha_c, inverse_c)
    own = jnp.concatenate([main[0], send(main[1], 0, 0, 1)], axis=0)
    cached = after(cached, own)
    added = pl.pallas_call(
        cached_kernel,
        grid=(1,),
        in_specs=[whole(depth, groups * past), whole(taps, depth, width)],
        out_specs=whole(groups * past, 128),
        out_shape=jax.ShapeDtypeStruct((groups * past, 128), BF16),
        scratch_shapes=[pltpu.VMEM((depth, 512), BF16), pltpu.VMEM((groups * past, 128), F32)],
        compiler_params=pltpu.CompilerParams(vmem_limit_bytes=VMEM_LIMIT),
        name="cached",
    )(cached, conv_in_w)
    every = lax.all_to_all(
        jnp.broadcast_to(added[None], (8,) + added.shape), "stream", 0, 0, tiled=True
    ).reshape(8 * groups * past, 128)
    low = jnp.concatenate([own, send(own, 1, 0)], axis=0)
    high = jnp.concatenate([send(own, 2, 0), send(own, 3, 0)], axis=0)
    up_low, down_low = send(low, 0, 1), send(low, 0, 3)
    up_high, down_high = send(high, 0, 1), send(high, 0, 3)
    far_low, far_high = send(up_low, 0, 1), send(down_high, 0, 3)
    columns = [low, high, up_low, up_high, far_low, far_high, down_low, down_high]

    head = pl.pallas_call(
        history_kernel,
        grid_spec=pltpu.PrefetchScalarGridSpec(
            num_scalar_prefetch=1,
            grid=(1,),
            in_specs=[
                whole(8 * groups * past, 128),
                whole(groups, 16, depth),
                whole(taps, depth, width),
                whole(1, 128),
                whole(1, 128),
            ],
            out_specs=whole(2, width, 128),
            scratch_shapes=[
                pltpu.VMEM((depth, 512), BF16),
                pltpu.VMEM((groups * past, 128), F32),
                pltpu.VMEM((8 * groups * past, 128), F32),
            ],
        ),
        out_shape=jax.ShapeDtypeStruct((2, width, 128), BF16),
        compiler_params=pltpu.CompilerParams(vmem_limit_bytes=VMEM_LIMIT),
        name="coarse_history",
    )(prev_slot, every, latents, conv_in_w, alpha_c, inverse_c)
    heads = lax.all_to_all(
        jnp.tile(head, (16, 1, 1)), "tm", 0, 0, tiled=True
    ).reshape(32 * width, 128)

    offsets = []
    for dy in range(4):
        for dz in range(4):
            for flip in range(2):
                source = ((z - dz) % 4) * 8 + ((y - dy) % 4) * 2 + (core + flip) % 2
                offsets.append(source * width)
    offsets = jnp.stack(offsets).astype(jnp.int32)
    n = half * frames
    blocks = pl.pallas_call(
        upsample_kernel,
        grid_spec=pltpu.PrefetchScalarGridSpec(
            num_scalar_prefetch=1,
            grid=(1,),
            in_specs=[whole(4 * width, n)] * 8
            + [whole(32 * width, 128), whole(16 * width, 32 * width)],
            out_specs=whole(32, 24, 8 * width),
            scratch_shapes=[
                pltpu.VMEM((32 * width, n), BF16),
                pltpu.VMEM((n + 8, 8 * width), F32),
            ],
        ),
        out_shape=jax.ShapeDtypeStruct((32, 24, 8 * width), BF16),
        compiler_params=pltpu.CompilerParams(vmem_limit_bytes=60 * 1024 * 1024),
        name="upsample",
    )(offsets, *columns, heads, up)
    arrived = lax.all_to_all(blocks, "tm", 0, 0, tiled=True)

    shard = 16
    rows = shard * groups
    limit = 8 * lengths - tm * shard
    limit = jnp.tile(limit, shard)[:, None].astype(jnp.int32)
    return pl.pallas_call(
        residual_kernel,
        grid=(1,),
        in_specs=[
            whole(32, 24, 8 * width),
            whole(rows, 1),
            whole(1, channels),
            whole(1, channels),
            whole(1, channels),
            whole(1, channels),
            pl.BlockSpec(memory_space=pl.ANY),
            whole(channels, channels),
        ],
        out_specs=whole(groups, shard, channels),
        out_shape=jax.ShapeDtypeStruct((groups, shard, channels), BF16),
        scratch_shapes=[
            pltpu.VMEM((24 * groups, channels), F32),
            pltpu.VMEM((24 * groups, channels), BF16),
            pltpu.VMEM((channels // 128, rows, 128), F32),
            pltpu.VMEM((taps, channels, channels), BF16),
            pltpu.SemaphoreType.DMA((taps,)),
        ],
        compiler_params=pltpu.CompilerParams(vmem_limit_bytes=VMEM_LIMIT),
        name="residual",
    )(
        arrived,
        limit,
        alpha_in[None],
        (1.0 / alpha_in)[None],
        alpha_mid[None],
        (1.0 / alpha_mid)[None],
        dilated,
        project_w,
    )


def solution(mesh):
    return jax.shard_map(
        per_device,
        mesh=mesh,
        in_specs=(
            P("stream", None, None),
            P("stream", None, "tm"),
            P("stream"),
            P("stream"),
            P(None, None, "tm"),
            P(None, None, "tm"),
            P("tm"),
            P(),
            P(),
            P(None, "tm", None),
            P(),
        ),
        out_specs=P("stream", "tm", None),
        check_vma=False,
    )
```

```python
import functools

import jax
import jax.numpy as jnp
from jax import lax
from jax.experimental import pallas as pl
from jax.experimental.pallas import tpu as pltpu
from jax.sharding import PartitionSpec as P

F32 = jnp.float32
BF16 = jnp.bfloat16
VMEM_LIMIT = 48 * 1024 * 1024


def sin_squared(u):
    k = jnp.floor(u * 0.3183098861837907 + 0.5)
    r = u - k * 3.140625
    r = r - k * 0.0009670257568359375
    r = r - k * 6.2771141529083252e-07
    r = jnp.clip(r, -1.5708, 1.5708)
    q = r * r
    p = -2.5052108385441720e-08
    p = p * q + 2.7557319223985893e-06
    p = p * q - 1.9841269841269841e-04
    p = p * q + 8.3333333333333333e-03
    p = p * q - 1.6666666666666667e-01
    s = r + r * (q * p)
    return s * s


def snake(x, alpha, inverse):
    return x + sin_squared(alpha * x) * inverse


def fill_taps(w_ref, wc_ref):
    taps, _, width = w_ref.shape
    wc_ref[...] = jnp.zeros_like(wc_ref)
    for k in range(taps):
        at = 64 * k
        wc_ref[:, at : at + width] = w_ref[k]


def tap_sum(y, shift, width):
    rows = y.shape[0]
    total = None
    for g in range(y.shape[1] // 128):
        part = y[:, 128 * g : 128 * g + 128]
        turn = (-(2 * g + shift)) % rows
        if turn:
            part = pltpu.roll(part, turn, 0)
        total = part if total is None else total + part
    odd = pltpu.roll(pltpu.roll(total, rows - 1, 0), 64, 1)
    return total + odd


def coarse_kernel(
    order_ref, lat_ref, w_ref, a_ref, ia_ref, out_ref, first_ref, wc_ref, v_ref
):
    half, frames, depth = lat_ref.shape
    width = out_ref.shape[1]

    @pl.when(pl.program_id(0) == 0)
    def _():
        fill_taps(w_ref, wc_ref)

    x = lat_ref[...].reshape(half * frames, depth)
    y = jnp.dot(x, wc_ref[...], preferred_element_type=F32)
    past = first_ref.shape[0] // half
    blank = jnp.zeros((past, y.shape[1]), F32)
    for s in range(half):
        ys = y[s * frames : (s + 1) * frames]
        v_ref[s * frames : (s + 1) * frames, :] = tap_sum(ys, -6, width)
        first_ref[past * s : past * (s + 1), :] = tap_sum(
            jnp.concatenate([blank, ys[:past]], axis=0), 0, width
        )[:past]
    u = [v_ref[pl.ds(t, half, stride=frames), :] for t in range(frames)]
    u = jnp.concatenate(u, axis=0)
    u = snake(u, a_ref[...], ia_ref[...])
    out_ref[0] = u.T[:width].astype(BF16)


def cached_kernel(h_ref, w_ref, out_ref, wc_ref, v_ref):
    fill_taps(w_ref, wc_ref)
    rows = h_ref.shape[1]
    past = 8
    ht = h_ref[...].astype(F32).T.astype(BF16)
    y = jnp.dot(ht, wc_ref[...], preferred_element_type=F32)
    blank = jnp.zeros((past, y.shape[1]), F32)
    for s in range(rows // past):
        z = jnp.concatenate([y[past * s : past * (s + 1)], blank], axis=0)
        v_ref[past * s : past * (s + 1), :] = tap_sum(z, 0, 48)[:past]
    out_ref[...] = v_ref[...].astype(BF16)


def history_kernel(
    slot_ref, c_ref, first_ref, a_ref, ia_ref, out_ref, v_ref, all_ref
):
    width = out_ref.shape[1]
    past = 8
    streams = first_ref.shape[0] // past
    half = streams // 2
    all_ref[...] = c_ref[...].astype(F32)
    for s in range(streams):
        at = pl.multiple_of(slot_ref[s] * past, past)
        mine = slice(past * s, past * (s + 1))
        v_ref[mine, :] = first_ref[mine, :] + all_ref[pl.ds(at, past), :]
    for c in range(2):
        rows = [
            v_ref[pl.ds(c * half * past + i, half, stride=past), :] for i in range(past)
        ]
        gap = jnp.zeros((128 - past * half, 128), F32)
        u = jnp.concatenate(rows[2:] + [gap] + rows[:2], axis=0)
        u = snake(u, a_ref[...], ia_ref[...])
        out_ref[c] = u.T[:width].astype(BF16)


def upsample_kernel(off_ref, *refs):
    x_refs, (xh_ref, w_ref, out_ref, xs_ref, fs_ref) = refs[:8], refs[8:]
    width = 48
    n = xs_ref.shape[1]
    pieces = x_refs[0].shape[0] // width
    for part, ref in enumerate(x_refs):
        for i in range(pieces):
            at = pl.multiple_of(off_ref[part * pieces + i], 16)
            xs_ref[pl.ds(at, width), :] = ref[i * width : (i + 1) * width, :]
    rows = w_ref.shape[0]
    half = rows // 2
    r = jnp.dot(w_ref[...], xs_ref[...], preferred_element_type=F32)
    rh = jnp.dot(w_ref[...], xh_ref[...], preferred_element_type=F32)
    lane = lax.broadcasted_iota(jnp.int32, (rows, 128), 1)
    first = jnp.where(lane < 48, rh, r[:, :128])
    r = jnp.concatenate([first, r[:, 128:]], axis=1)
    turned = pltpu.roll(rh[half:], 8, 1)
    shifted = pltpu.roll(r[half:], 8, 1)
    lane = lax.broadcasted_iota(jnp.int32, (half, 128), 1)
    shifted = jnp.concatenate(
        [jnp.where(lane < 8, turned, shifted[:, :128]), shifted[:, 128:]], axis=1
    )
    fs_ref[8 : 8 + n, :] = (r[:half] + shifted).T
    fs_ref[0:8, :] = (rh[:half] + turned).T[120:128]
    blocks, take, _ = out_ref.shape
    for b in range(blocks):
        out_ref[b] = fs_ref[16 * b : 16 * b + take, :].astype(BF16)


def residual_kernel(
    arr_ref, lim_ref, ai_ref, iai_ref, am_ref, iam_ref, wd_hbm, wp_ref,
    out_ref, f_ref, win_ref, r_ref, wd_ref, sems,
):
    streams, shard, channels = out_ref.shape
    rows = streams * shard
    sources, take, _ = arr_ref.shape
    taps = wd_ref.shape[0]
    piece = 48
    half = streams // 2
    copies = [
        pltpu.make_async_copy(wd_hbm.at[k], wd_ref.at[k], sems.at[k])
        for k in range(taps)
    ]
    for copy in copies:
        copy.start()
    for c in range(2):
        for j in range(8):
            x = jnp.concatenate(
                [
                    arr_ref[m, :, piece * j : piece * (j + 1)].astype(F32)
                    for m in range(c, sources, 2)
                ],
                axis=1,
            )
            for t in range(take // half):
                at = (8 * t + j) * streams + half * c
                f_ref[at : at + half, :] = x[half * t : half * (t + 1)]
    used = 2 * streams
    win_ref[used:, :] = snake(f_ref[used:, :], ai_ref[...], iai_ref[...]).astype(BF16)
    total = None
    for k in range(taps):
        copies[k].wait()
        at = (k + 2) * streams
        part = jnp.dot(
            win_ref[at : at + rows, :], wd_ref[k], preferred_element_type=F32
        )
        total = part if total is None else total + part
    middle = snake(total, am_ref[...], iam_ref[...]).astype(BF16)
    summed = f_ref[8 * streams :, :] + jnp.dot(
        middle, wp_ref[...], preferred_element_type=F32
    )
    local = lax.broadcasted_iota(jnp.int32, (rows, channels), 0) // streams
    kept = jnp.where(local < lim_ref[...], summed, 0.0)
    for g in range(channels // 128):
        r_ref[g] = kept[:, 128 * g : 128 * (g + 1)]
    for s in range(streams):
        out_ref[s] = jnp.concatenate(
            [
                r_ref[g, pl.ds(s, shard, stride=streams), :]
                for g in range(channels // 128)
            ],
            axis=1,
        ).astype(BF16)


def after(x, *others):
    return lax.optimization_barrier((x,) + others)[0]


def whole(*shape):
    return pl.BlockSpec(shape, lambda *_: (0,) * len(shape))


def per_device(
    latents,
    cache_prev,
    prev_slot,
    lengths,
    conv_in_w,
    upsample_w,
    alpha_coarse,
    alpha_in,
    alpha_mid,
    dilated_w,
    project_w,
):
    groups, frames, depth = latents.shape
    taps, _, width = conv_in_w.shape
    past = cache_prev.shape[1]
    slab = cache_prev.shape[2]
    half = groups // 2
    channels = dilated_w.shape[2]
    tm = lax.axis_index("tm")
    z, y, core = tm // 8, (tm // 2) % 4, tm % 2

    def turned(dz, dy, flip=0):
        pairs = []
        for m in range(32):
            a, b, c = m // 8, (m // 2) % 4, m % 2
            pairs.append((m, ((a + dz) % 4) * 8 + ((b + dy) % 4) * 2 + (c + flip) % 2))
        return pairs

    def send(x, dz, dy, flip=0):
        return lax.ppermute(x, "tm", turned(dz, dy, flip))

    dilated = lax.all_gather(dilated_w, "tm", axis=1, tiled=True)
    up_t = jnp.transpose(upsample_w, (0, 2, 1))
    up_other = send(up_t, 0, 0, 1)
    up = jnp.where(
        core == 0,
        jnp.concatenate([up_t, up_other], axis=1),
        jnp.concatenate([up_other, up_t], axis=1),
    ).reshape(-1, up_t.shape[2])

    flat = jnp.transpose(cache_prev, (2, 0, 1)).reshape(slab, groups * past)
    cached = lax.all_to_all(
        jnp.broadcast_to(flat[None], (32,) + flat.shape), "tm", 0, 0, tiled=True
    ).reshape(32 * slab, groups * past)
    pad = 128 - width
    alpha_c = jnp.pad(alpha_coarse, (0, pad), constant_values=1.0)[None]
    inverse_c = 1.0 / alpha_c
    order = jnp.stack([core, 1 - core]).astype(jnp.int32)
    main, first = pl.pallas_call(
        coarse_kernel,
        grid_spec=pltpu.PrefetchScalarGridSpec(
            num_scalar_prefetch=1,
            grid=(2,),
            in_specs=[
                pl.BlockSpec((half, frames, depth), lambda i, o: (o[i], 0, 0)),
                whole(taps, depth, width),
                whole(1, 128),
                whole(1, 128),
            ],
            out_specs=[
                pl.BlockSpec((1, width, half * frames), lambda i, o: (i, 0, 0)),
                pl.BlockSpec((half * past, 128), lambda i, o: (o[i], 0)),
            ],
            scratch_shapes=[
                pltpu.VMEM((depth, 512), BF16),
                pltpu.VMEM((half * frames, 128), F32),
            ],
        ),
        out_shape=[
            jax.ShapeDtypeStruct((2, width, half * frames), BF16),
            jax.ShapeDtypeStruct((groups * past, 128), F32),
        ],
        compiler_params=pltpu.CompilerParams(vmem_limit_bytes=VMEM_LIMIT),
        name="coarse_main",
    )(order, latents, conv_in_w, alpha_c, inverse_c)
    own = jnp.concatenate([main[0], send(main[1], 0, 0, 1)], axis=0)
    cached = after(cached, own)
    added = pl.pallas_call(
        cached_kernel,
        grid=(1,),
        in_specs=[whole(depth, groups * past), whole(taps, depth, width)],
        out_specs=whole(groups * past, 128),
        out_shape=jax.ShapeDtypeStruct((groups * past, 128), BF16),
        scratch_shapes=[pltpu.VMEM((depth, 512), BF16), pltpu.VMEM((groups * past, 128), F32)],
        compiler_params=pltpu.CompilerParams(vmem_limit_bytes=VMEM_LIMIT),
        name="cached",
    )(cached, conv_in_w)
    every = lax.all_to_all(
        jnp.broadcast_to(added[None], (8,) + added.shape), "stream", 0, 0, tiled=True
    ).reshape(8 * groups * past, 128)
    low = jnp.concatenate([own, send(own, 1, 0)], axis=0)
    high = jnp.concatenate([send(own, 2, 0), send(own, 3, 0)], axis=0)
    up_low, down_low = send(low, 0, 1), send(low, 0, 3)
    up_high, down_high = send(high, 0, 1), send(high, 0, 3)
    far_low, far_high = send(up_low, 0, 1), send(down_high, 0, 3)
    columns = [low, high, up_low, up_high, far_low, far_high, down_low, down_high]

    head = pl.pallas_call(
        history_kernel,
        grid_spec=pltpu.PrefetchScalarGridSpec(
            num_scalar_prefetch=1,
            grid=(1,),
            in_specs=[
                whole(8 * groups * past, 128),
                whole(groups * past, 128),
                whole(1, 128),
                whole(1, 128),
            ],
            out_specs=whole(2, width, 128),
            scratch_shapes=[
                pltpu.VMEM((groups * past, 128), F32),
                pltpu.VMEM((8 * groups * past, 128), F32),
            ],
        ),
        out_shape=jax.ShapeDtypeStruct((2, width, 128), BF16),
        compiler_params=pltpu.CompilerParams(vmem_limit_bytes=VMEM_LIMIT),
        name="coarse_history",
    )(prev_slot, every, first, alpha_c, inverse_c)
    heads = lax.all_to_all(
        jnp.tile(head, (16, 1, 1)), "tm", 0, 0, tiled=True
    ).reshape(32 * width, 128)

    offsets = []
    for dy in range(4):
        for dz in range(4):
            for flip in range(2):
                source = ((z - dz) % 4) * 8 + ((y - dy) % 4) * 2 + (core + flip) % 2
                offsets.append(source * width)
    offsets = jnp.stack(offsets).astype(jnp.int32)
    n = half * frames
    blocks = pl.pallas_call(
        upsample_kernel,
        grid_spec=pltpu.PrefetchScalarGridSpec(
            num_scalar_prefetch=1,
            grid=(1,),
            in_specs=[whole(4 * width, n)] * 8
            + [whole(32 * width, 128), whole(16 * width, 32 * width)],
            out_specs=whole(32, 24, 8 * width),
            scratch_shapes=[
                pltpu.VMEM((32 * width, n), BF16),
                pltpu.VMEM((n + 8, 8 * width), F32),
            ],
        ),
        out_shape=jax.ShapeDtypeStruct((32, 24, 8 * width), BF16),
        compiler_params=pltpu.CompilerParams(vmem_limit_bytes=60 * 1024 * 1024),
        name="upsample",
    )(offsets, *columns, heads, up)
    arrived = lax.all_to_all(blocks, "tm", 0, 0, tiled=True)

    shard = 16
    rows = shard * groups
    limit = 8 * lengths - tm * shard
    limit = jnp.tile(limit, shard)[:, None].astype(jnp.int32)
    return pl.pallas_call(
        residual_kernel,
        grid=(1,),
        in_specs=[
            whole(32, 24, 8 * width),
            whole(rows, 1),
            whole(1, channels),
            whole(1, channels),
            whole(1, channels),
            whole(1, channels),
            pl.BlockSpec(memory_space=pl.ANY),
            whole(channels, channels),
        ],
        out_specs=whole(groups, shard, channels),
        out_shape=jax.ShapeDtypeStruct((groups, shard, channels), BF16),
        scratch_shapes=[
            pltpu.VMEM((24 * groups, channels), F32),
            pltpu.VMEM((24 * groups, channels), BF16),
            pltpu.VMEM((channels // 128, rows, 128), F32),
            pltpu.VMEM((taps, channels, channels), BF16),
            pltpu.SemaphoreType.DMA((taps,)),
        ],
        compiler_params=pltpu.CompilerParams(vmem_limit_bytes=VMEM_LIMIT),
        name="residual",
    )(
        arrived,
        limit,
        alpha_in[None],
        (1.0 / alpha_in)[None],
        alpha_mid[None],
        (1.0 / alpha_mid)[None],
        dilated,
        project_w,
    )


def solution(mesh):
    return jax.shard_map(
        per_device,
        mesh=mesh,
        in_specs=(
            P("stream", None, None),
            P("stream", None, "tm"),
            P("stream"),
            P("stream"),
            P(None, None, "tm"),
            P(None, None, "tm"),
            P("tm"),
            P(),
            P(),
            P(None, "tm", None),
            P(),
        ),
        out_specs=P("stream", "tm", None),
        check_vma=False,
    )
```

```python
import functools

import jax
import jax.numpy as jnp
from jax import lax
from jax.experimental import pallas as pl
from jax.experimental.pallas import tpu as pltpu
from jax.sharding import PartitionSpec as P

F32 = jnp.float32
BF16 = jnp.bfloat16
VMEM_LIMIT = 48 * 1024 * 1024


def sin_squared(u):
    k = jnp.floor(u * 0.3183098861837907 + 0.5)
    r = u - k * 3.140625
    r = r - k * 0.0009670257568359375
    r = r - k * 6.2771141529083252e-07
    r = jnp.clip(r, -1.5708, 1.5708)
    q = r * r
    p = -2.5052108385441720e-08
    p = p * q + 2.7557319223985893e-06
    p = p * q - 1.9841269841269841e-04
    p = p * q + 8.3333333333333333e-03
    p = p * q - 1.6666666666666667e-01
    s = r + r * (q * p)
    return s * s


def snake(x, alpha, inverse):
    return x + sin_squared(alpha * x) * inverse


def fill_taps(w_ref, wc_ref):
    taps, _, width = w_ref.shape
    wc_ref[...] = jnp.zeros_like(wc_ref)
    for k in range(taps):
        at = 64 * k
        wc_ref[:, at : at + width] = w_ref[k]


def tap_sum(y, shift, width):
    rows = y.shape[0]
    total = None
    for g in range(y.shape[1] // 128):
        part = y[:, 128 * g : 128 * g + 128]
        turn = (-(2 * g + shift)) % rows
        if turn:
            part = pltpu.roll(part, turn, 0)
        total = part if total is None else total + part
    odd = pltpu.roll(pltpu.roll(total, rows - 1, 0), 64, 1)
    return total + odd


def coarse_kernel(
    order_ref, lat_ref, w_ref, a_ref, ia_ref, out_ref, first_ref, wc_ref, v_ref
):
    half, frames, depth = lat_ref.shape
    width = out_ref.shape[1]

    @pl.when(pl.program_id(0) == 0)
    def _():
        fill_taps(w_ref, wc_ref)

    x = lat_ref[...].reshape(half * frames, depth)
    y = jnp.dot(x, wc_ref[...], preferred_element_type=F32)
    past = first_ref.shape[0] // half
    blank = jnp.zeros((past, y.shape[1]), F32)
    for s in range(half):
        ys = y[s * frames : (s + 1) * frames]
        v_ref[s * frames : (s + 1) * frames, :] = tap_sum(ys, -6, width)
        first_ref[past * s : past * (s + 1), :] = tap_sum(
            jnp.concatenate([blank, ys[:past]], axis=0), 0, width
        )[:past]
    u = [v_ref[pl.ds(t, half, stride=frames), :] for t in range(frames)]
    u = jnp.concatenate(u, axis=0)
    u = snake(u, a_ref[...], ia_ref[...])
    out_ref[0] = u.T[:width].astype(BF16)


def cached_kernel(h_ref, w_ref, out_ref, wc_ref, v_ref):
    fill_taps(w_ref, wc_ref)
    rows = h_ref.shape[1]
    past = 8
    ht = h_ref[...].astype(F32).T.astype(BF16)
    y = jnp.dot(ht, wc_ref[...], preferred_element_type=F32)
    blank = jnp.zeros((past, y.shape[1]), F32)
    for s in range(rows // past):
        z = jnp.concatenate([y[past * s : past * (s + 1)], blank], axis=0)
        v_ref[past * s : past * (s + 1), :] = tap_sum(z, 0, 48)[:past]
    part = v_ref[...].astype(BF16)
    for group in range(out_ref.shape[0]):
        out_ref[group] = part


def history_kernel(
    slot_ref, c_ref, first_ref, a_ref, ia_ref, out_ref, v_ref, all_ref
):
    width = out_ref.shape[1]
    past = 8
    streams = first_ref.shape[0] // past
    half = streams // 2
    all_ref[...] = c_ref[...].astype(F32)
    for s in range(streams):
        at = pl.multiple_of(slot_ref[s] * past, past)
        mine = slice(past * s, past * (s + 1))
        v_ref[mine, :] = first_ref[mine, :] + all_ref[pl.ds(at, past), :]
    for c in range(2):
        rows = [
            v_ref[pl.ds(c * half * past + i, half, stride=past), :] for i in range(past)
        ]
        gap = jnp.zeros((128 - past * half, 128), F32)
        u = jnp.concatenate(rows[2:] + [gap] + rows[:2], axis=0)
        u = snake(u, a_ref[...], ia_ref[...])
        part = u.T[:width].astype(BF16)
        for m in range(c, out_ref.shape[0], 2):
            out_ref[m] = part


def upsample_kernel(off_ref, *refs):
    x_refs, (xh_ref, w_ref, out_ref, xs_ref, fs_ref) = refs[:8], refs[8:]
    width = 48
    n = xs_ref.shape[1]
    pieces = x_refs[0].shape[0] // width
    for part, ref in enumerate(x_refs):
        for i in range(pieces):
            at = pl.multiple_of(off_ref[part * pieces + i], 16)
            xs_ref[pl.ds(at, width), :] = ref[i * width : (i + 1) * width, :]
    rows = w_ref.shape[0]
    half = rows // 2
    r = jnp.dot(w_ref[...], xs_ref[...], preferred_element_type=F32)
    rh = jnp.dot(w_ref[...], xh_ref[...], preferred_element_type=F32)
    lane = lax.broadcasted_iota(jnp.int32, (rows, 128), 1)
    first = jnp.where(lane < 48, rh, r[:, :128])
    r = jnp.concatenate([first, r[:, 128:]], axis=1)
    turned = pltpu.roll(rh[half:], 8, 1)
    shifted = pltpu.roll(r[half:], 8, 1)
    lane = lax.broadcasted_iota(jnp.int32, (half, 128), 1)
    shifted = jnp.concatenate(
        [jnp.where(lane < 8, turned, shifted[:, :128]), shifted[:, 128:]], axis=1
    )
    fs_ref[8 : 8 + n, :] = (r[:half] + shifted).T
    fs_ref[0:8, :] = (rh[:half] + turned).T[120:128]
    blocks, take, _ = out_ref.shape
    for b in range(blocks):
        out_ref[b] = fs_ref[16 * b : 16 * b + take, :].astype(BF16)


def residual_kernel(
    arr_ref, lim_ref, ai_ref, iai_ref, am_ref, iam_ref, wd_hbm, wp_ref,
    out_ref, f_ref, win_ref, r_ref, wd_ref, sems,
):
    streams, shard, channels = out_ref.shape
    rows = streams * shard
    sources, take, _ = arr_ref.shape
    taps = wd_ref.shape[0]
    piece = 48
    half = streams // 2
    copies = [
        pltpu.make_async_copy(wd_hbm.at[k], wd_ref.at[k], sems.at[k])
        for k in range(taps)
    ]
    for copy in copies:
        copy.start()
    for c in range(2):
        for j in range(8):
            x = jnp.concatenate(
                [
                    arr_ref[m, :, piece * j : piece * (j + 1)].astype(F32)
                    for m in range(c, sources, 2)
                ],
                axis=1,
            )
            for t in range(take // half):
                at = (8 * t + j) * streams + half * c
                f_ref[at : at + half, :] = x[half * t : half * (t + 1)]
    used = 2 * streams
    win_ref[used:, :] = snake(f_ref[used:, :], ai_ref[...], iai_ref[...]).astype(BF16)
    total = None
    for k in range(taps):
        copies[k].wait()
        at = (k + 2) * streams
        part = jnp.dot(
            win_ref[at : at + rows, :], wd_ref[k], preferred_element_type=F32
        )
        total = part if total is None else total + part
    middle = snake(total, am_ref[...], iam_ref[...]).astype(BF16)
    summed = f_ref[8 * streams :, :] + jnp.dot(
        middle, wp_ref[...], preferred_element_type=F32
    )
    local = lax.broadcasted_iota(jnp.int32, (rows, channels), 0) // streams
    kept = jnp.where(local < lim_ref[...], summed, 0.0)
    for g in range(channels // 128):
        r_ref[g] = kept[:, 128 * g : 128 * (g + 1)]
    for s in range(streams):
        out_ref[s] = jnp.concatenate(
            [
                r_ref[g, pl.ds(s, shard, stride=streams), :]
                for g in range(channels // 128)
            ],
            axis=1,
        ).astype(BF16)


def after(x, *others):
    return lax.optimization_barrier((x,) + others)[0]


def whole(*shape):
    return pl.BlockSpec(shape, lambda *_: (0,) * len(shape))


def per_device(
    latents,
    cache_prev,
    prev_slot,
    lengths,
    conv_in_w,
    upsample_w,
    alpha_coarse,
    alpha_in,
    alpha_mid,
    dilated_w,
    project_w,
):
    groups, frames, depth = latents.shape
    taps, _, width = conv_in_w.shape
    past = cache_prev.shape[1]
    slab = cache_prev.shape[2]
    half = groups // 2
    channels = dilated_w.shape[2]
    tm = lax.axis_index("tm")
    z, y, core = tm // 8, (tm // 2) % 4, tm % 2

    def turned(dz, dy, flip=0):
        pairs = []
        for m in range(32):
            a, b, c = m // 8, (m // 2) % 4, m % 2
            pairs.append((m, ((a + dz) % 4) * 8 + ((b + dy) % 4) * 2 + (c + flip) % 2))
        return pairs

    def send(x, dz, dy, flip=0):
        return lax.ppermute(x, "tm", turned(dz, dy, flip))

    dilated = lax.all_gather(dilated_w, "tm", axis=1, tiled=True)
    up_t = jnp.transpose(upsample_w, (0, 2, 1))
    up_other = send(up_t, 0, 0, 1)
    up = jnp.where(
        core == 0,
        jnp.concatenate([up_t, up_other], axis=1),
        jnp.concatenate([up_other, up_t], axis=1),
    ).reshape(-1, up_t.shape[2])

    flat = jnp.transpose(cache_prev, (2, 0, 1)).reshape(slab, groups * past)
    cached = lax.all_to_all(
        jnp.broadcast_to(flat[None], (32,) + flat.shape), "tm", 0, 0, tiled=True
    ).reshape(32 * slab, groups * past)
    pad = 128 - width
    alpha_c = jnp.pad(alpha_coarse, (0, pad), constant_values=1.0)[None]
    inverse_c = 1.0 / alpha_c
    order = jnp.stack([core, 1 - core]).astype(jnp.int32)
    main, first = pl.pallas_call(
        coarse_kernel,
        grid_spec=pltpu.PrefetchScalarGridSpec(
            num_scalar_prefetch=1,
            grid=(2,),
            in_specs=[
                pl.BlockSpec((half, frames, depth), lambda i, o: (o[i], 0, 0)),
                whole(taps, depth, width),
                whole(1, 128),
                whole(1, 128),
            ],
            out_specs=[
                pl.BlockSpec((1, width, half * frames), lambda i, o: (i, 0, 0)),
                pl.BlockSpec((half * past, 128), lambda i, o: (o[i], 0)),
            ],
            scratch_shapes=[
                pltpu.VMEM((depth, 512), BF16),
                pltpu.VMEM((half * frames, 128), F32),
            ],
        ),
        out_shape=[
            jax.ShapeDtypeStruct((2, width, half * frames), BF16),
            jax.ShapeDtypeStruct((groups * past, 128), F32),
        ],
        compiler_params=pltpu.CompilerParams(vmem_limit_bytes=VMEM_LIMIT),
        name="coarse_main",
    )(order, latents, conv_in_w, alpha_c, inverse_c)
    own = jnp.concatenate([main[0], send(main[1], 0, 0, 1)], axis=0)
    cached = after(cached, own)
    added = pl.pallas_call(
        cached_kernel,
        grid=(1,),
        in_specs=[whole(depth, groups * past), whole(taps, depth, width)],
        out_specs=whole(8, groups * past, 128),
        out_shape=jax.ShapeDtypeStruct((8, groups * past, 128), BF16),
        scratch_shapes=[pltpu.VMEM((depth, 512), BF16), pltpu.VMEM((groups * past, 128), F32)],
        compiler_params=pltpu.CompilerParams(vmem_limit_bytes=VMEM_LIMIT),
        name="cached",
    )(cached, conv_in_w)
    every = lax.all_to_all(added, "stream", 0, 0, tiled=True).reshape(8 * groups * past, 128)
    low = jnp.concatenate([own, send(own, 1, 0)], axis=0)
    high = jnp.concatenate([send(own, 2, 0), send(own, 3, 0)], axis=0)
    up_low, down_low = send(low, 0, 1), send(low, 0, 3)
    up_high, down_high = send(high, 0, 1), send(high, 0, 3)
    far_low, far_high = send(up_low, 0, 1), send(down_high, 0, 3)
    columns = [low, high, up_low, up_high, far_low, far_high, down_low, down_high]

    head = pl.pallas_call(
        history_kernel,
        grid_spec=pltpu.PrefetchScalarGridSpec(
            num_scalar_prefetch=1,
            grid=(1,),
            in_specs=[
                whole(8 * groups * past, 128),
                whole(groups * past, 128),
                whole(1, 128),
                whole(1, 128),
            ],
            out_specs=whole(32, width, 128),
            scratch_shapes=[
                pltpu.VMEM((groups * past, 128), F32),
                pltpu.VMEM((8 * groups * past, 128), F32),
            ],
        ),
        out_shape=jax.ShapeDtypeStruct((32, width, 128), BF16),
        compiler_params=pltpu.CompilerParams(vmem_limit_bytes=VMEM_LIMIT),
        name="coarse_history",
    )(prev_slot, every, first, alpha_c, inverse_c)
    heads = lax.all_to_all(head, "tm", 0, 0, tiled=True).reshape(32 * width, 128)

    offsets = []
    for dy in range(4):
        for dz in range(4):
            for flip in range(2):
                source = ((z - dz) % 4) * 8 + ((y - dy) % 4) * 2 + (core + flip) % 2
                offsets.append(source * width)
    offsets = jnp.stack(offsets).astype(jnp.int32)
    n = half * frames
    blocks = pl.pallas_call(
        upsample_kernel,
        grid_spec=pltpu.PrefetchScalarGridSpec(
            num_scalar_prefetch=1,
            grid=(1,),
            in_specs=[whole(4 * width, n)] * 8
            + [whole(32 * width, 128), whole(16 * width, 32 * width)],
            out_specs=whole(32, 24, 8 * width),
            scratch_shapes=[
                pltpu.VMEM((32 * width, n), BF16),
                pltpu.VMEM((n + 8, 8 * width), F32),
            ],
        ),
        out_shape=jax.ShapeDtypeStruct((32, 24, 8 * width), BF16),
        compiler_params=pltpu.CompilerParams(vmem_limit_bytes=60 * 1024 * 1024),
        name="upsample",
    )(offsets, *columns, heads, up)
    arrived = lax.all_to_all(blocks, "tm", 0, 0, tiled=True)

    shard = 16
    rows = shard * groups
    limit = 8 * lengths - tm * shard
    limit = jnp.tile(limit, shard)[:, None].astype(jnp.int32)
    return pl.pallas_call(
        residual_kernel,
        grid=(1,),
        in_specs=[
            whole(32, 24, 8 * width),
            whole(rows, 1),
            whole(1, channels),
            whole(1, channels),
            whole(1, channels),
            whole(1, channels),
            pl.BlockSpec(memory_space=pl.ANY),
            whole(channels, channels),
        ],
        out_specs=whole(groups, shard, channels),
        out_shape=jax.ShapeDtypeStruct((groups, shard, channels), BF16),
        scratch_shapes=[
            pltpu.VMEM((24 * groups, channels), F32),
            pltpu.VMEM((24 * groups, channels), BF16),
            pltpu.VMEM((channels // 128, rows, 128), F32),
            pltpu.VMEM((taps, channels, channels), BF16),
            pltpu.SemaphoreType.DMA((taps,)),
        ],
        compiler_params=pltpu.CompilerParams(vmem_limit_bytes=VMEM_LIMIT),
        name="residual",
    )(
        arrived,
        limit,
        alpha_in[None],
        (1.0 / alpha_in)[None],
        alpha_mid[None],
        (1.0 / alpha_mid)[None],
        dilated,
        project_w,
    )


def solution(mesh):
    return jax.shard_map(
        per_device,
        mesh=mesh,
        in_specs=(
            P("stream", None, None),
            P("stream", None, "tm"),
            P("stream"),
            P("stream"),
            P(None, None, "tm"),
            P(None, None, "tm"),
            P("tm"),
            P(),
            P(),
            P(None, "tm", None),
            P(),
        ),
        out_specs=P("stream", "tm", None),
        check_vma=False,
    )
```

```python
import functools

import jax
import jax.numpy as jnp
from jax import lax
from jax.experimental import pallas as pl
from jax.experimental.pallas import tpu as pltpu
from jax.sharding import PartitionSpec as P

F32 = jnp.float32
BF16 = jnp.bfloat16
VMEM_LIMIT = 48 * 1024 * 1024


def sin_squared(u):
    k = jnp.floor(u * 0.3183098861837907 + 0.5)
    r = u - k * 3.140625
    r = r - k * 0.0009670257568359375
    r = r - k * 6.2771141529083252e-07
    r = jnp.clip(r, -1.5708, 1.5708)
    q = r * r
    p = -2.5052108385441720e-08
    p = p * q + 2.7557319223985893e-06
    p = p * q - 1.9841269841269841e-04
    p = p * q + 8.3333333333333333e-03
    p = p * q - 1.6666666666666667e-01
    s = r + r * (q * p)
    return s * s


def snake(x, alpha, inverse):
    return x + sin_squared(alpha * x) * inverse


def fill_taps(w_ref, wc_ref):
    taps, _, width = w_ref.shape
    wc_ref[...] = jnp.zeros_like(wc_ref)
    for k in range(taps):
        at = 64 * k
        wc_ref[:, at : at + width] = w_ref[k]


def tap_sum(y, shift, width):
    rows = y.shape[0]
    total = None
    for g in range(y.shape[1] // 128):
        part = y[:, 128 * g : 128 * g + 128]
        turn = (-(2 * g + shift)) % rows
        if turn:
            part = pltpu.roll(part, turn, 0)
        total = part if total is None else total + part
    odd = pltpu.roll(pltpu.roll(total, rows - 1, 0), 64, 1)
    return total + odd


def coarse_kernel(
    order_ref, lat_ref, w_ref, a_ref, ia_ref, out_ref, first_ref, wc_ref, v_ref
):
    half, frames, depth = lat_ref.shape
    width = out_ref.shape[1]

    @pl.when(pl.program_id(0) == 0)
    def _():
        fill_taps(w_ref, wc_ref)

    x = lat_ref[...].reshape(half * frames, depth)
    y = jnp.dot(x, wc_ref[...], preferred_element_type=F32)
    past = first_ref.shape[0] // half
    blank = jnp.zeros((past, y.shape[1]), F32)
    for s in range(half):
        ys = y[s * frames : (s + 1) * frames]
        v_ref[s * frames : (s + 1) * frames, :] = tap_sum(ys, -6, width)
        first_ref[past * s : past * (s + 1), :] = tap_sum(
            jnp.concatenate([blank, ys[:past]], axis=0), 0, width
        )[:past]
    u = [v_ref[pl.ds(t, half, stride=frames), :] for t in range(frames)]
    u = jnp.concatenate(u, axis=0)
    u = snake(u, a_ref[...], ia_ref[...])
    out_ref[0] = u.T[:width].astype(BF16)


def cached_kernel(h_ref, w_ref, out_ref, wc_ref, v_ref):
    fill_taps(w_ref, wc_ref)
    rows = h_ref.shape[1]
    past = 8
    ht = h_ref[...].astype(F32).T.astype(BF16)
    y = jnp.dot(ht, wc_ref[...], preferred_element_type=F32)
    blank = jnp.zeros((past, y.shape[1]), F32)
    for s in range(rows // past):
        z = jnp.concatenate([y[past * s : past * (s + 1)], blank], axis=0)
        v_ref[past * s : past * (s + 1), :] = tap_sum(z, 0, 48)[:past]
    packed = out_ref.shape[0]
    lane = lax.broadcasted_iota(jnp.int32, (packed, 128), 1)
    upper = pltpu.roll(v_ref[packed:, :], 64, 1)
    out_ref[...] = jnp.where(lane < 64, v_ref[:packed, :], upper).astype(BF16)


def history_kernel(
    slot_ref, c_ref, first_ref, a_ref, ia_ref, out_ref, v_ref, all_ref
):
    width = out_ref.shape[1]
    past = 8
    streams = first_ref.shape[0] // past
    half = streams // 2
    all_ref[...] = c_ref[...].astype(F32)
    for s in range(streams):
        slot = slot_ref[s]
        at = pl.multiple_of(((slot >> 4) * 8 + (slot & 7)) * past, past)
        cached = all_ref[pl.ds(at, past), :]
        upper = ((slot >> 3) & 1) * jnp.ones((past, 128), jnp.int32)
        cached = jnp.where(upper == 1, pltpu.roll(cached, 64, 1), cached)
        mine = slice(past * s, past * (s + 1))
        v_ref[mine, :] = first_ref[mine, :] + cached
    for c in range(2):
        rows = [
            v_ref[pl.ds(c * half * past + i, half, stride=past), :] for i in range(past)
        ]
        gap = jnp.zeros((128 - past * half, 128), F32)
        u = jnp.concatenate(rows[2:] + [gap] + rows[:2], axis=0)
        u = snake(u, a_ref[...], ia_ref[...])
        out_ref[c] = u.T[:width].astype(BF16)


def upsample_kernel(off_ref, *refs):
    x_refs, (xh_ref, w_ref, out_ref, xs_ref, fs_ref) = refs[:8], refs[8:]
    width = 48
    n = xs_ref.shape[1]
    pieces = x_refs[0].shape[0] // width
    for part, ref in enumerate(x_refs):
        for i in range(pieces):
            at = pl.multiple_of(off_ref[part * pieces + i], 16)
            xs_ref[pl.ds(at, width), :] = ref[i * width : (i + 1) * width, :]
    rows = w_ref.shape[0]
    half = rows // 2
    r = jnp.dot(w_ref[...], xs_ref[...], preferred_element_type=F32)
    rh = jnp.dot(w_ref[...], xh_ref[...], preferred_element_type=F32)
    lane = lax.broadcasted_iota(jnp.int32, (rows, 128), 1)
    first = jnp.where(lane < 48, rh, r[:, :128])
    r = jnp.concatenate([first, r[:, 128:]], axis=1)
    turned = pltpu.roll(rh[half:], 8, 1)
    shifted = pltpu.roll(r[half:], 8, 1)
    lane = lax.broadcasted_iota(jnp.int32, (half, 128), 1)
    shifted = jnp.concatenate(
        [jnp.where(lane < 8, turned, shifted[:, :128]), shifted[:, 128:]], axis=1
    )
    fs_ref[8 : 8 + n, :] = (r[:half] + shifted).T
    fs_ref[0:8, :] = (rh[:half] + turned).T[120:128]
    blocks, take, _ = out_ref.shape
    for b in range(blocks):
        out_ref[b] = fs_ref[16 * b : 16 * b + take, :].astype(BF16)


def residual_kernel(
    arr_ref, lim_ref, ai_ref, iai_ref, am_ref, iam_ref, wd_hbm, wp_ref,
    out_ref, f_ref, win_ref, r_ref, wd_ref, sems,
):
    streams, shard, channels = out_ref.shape
    rows = streams * shard
    sources, take, _ = arr_ref.shape
    taps = wd_ref.shape[0]
    piece = 48
    half = streams // 2
    copies = [
        pltpu.make_async_copy(wd_hbm.at[k], wd_ref.at[k], sems.at[k])
        for k in range(taps)
    ]
    for copy in copies:
        copy.start()
    for c in range(2):
        for j in range(8):
            x = jnp.concatenate(
                [
                    arr_ref[m, :, piece * j : piece * (j + 1)].astype(F32)
                    for m in range(c, sources, 2)
                ],
                axis=1,
            )
            for t in range(take // half):
                at = (8 * t + j) * streams + half * c
                f_ref[at : at + half, :] = x[half * t : half * (t + 1)]
    used = 2 * streams
    win_ref[used:, :] = snake(f_ref[used:, :], ai_ref[...], iai_ref[...]).astype(BF16)
    total = None
    for k in range(taps):
        copies[k].wait()
        at = (k + 2) * streams
        part = jnp.dot(
            win_ref[at : at + rows, :], wd_ref[k], preferred_element_type=F32
        )
        total = part if total is None else total + part
    middle = snake(total, am_ref[...], iam_ref[...]).astype(BF16)
    summed = f_ref[8 * streams :, :] + jnp.dot(
        middle, wp_ref[...], preferred_element_type=F32
    )
    local = lax.broadcasted_iota(jnp.int32, (rows, channels), 0) // streams
    kept = jnp.where(local < lim_ref[...], summed, 0.0)
    for g in range(channels // 128):
        r_ref[g] = kept[:, 128 * g : 128 * (g + 1)]
    for s in range(streams):
        out_ref[s] = jnp.concatenate(
            [
                r_ref[g, pl.ds(s, shard, stride=streams), :]
                for g in range(channels // 128)
            ],
            axis=1,
        ).astype(BF16)


def after(x, *others):
    return lax.optimization_barrier((x,) + others)[0]


def whole(*shape):
    return pl.BlockSpec(shape, lambda *_: (0,) * len(shape))


def per_device(
    latents,
    cache_prev,
    prev_slot,
    lengths,
    conv_in_w,
    upsample_w,
    alpha_coarse,
    alpha_in,
    alpha_mid,
    dilated_w,
    project_w,
):
    groups, frames, depth = latents.shape
    taps, _, width = conv_in_w.shape
    past = cache_prev.shape[1]
    slab = cache_prev.shape[2]
    half = groups // 2
    channels = dilated_w.shape[2]
    tm = lax.axis_index("tm")
    z, y, core = tm // 8, (tm // 2) % 4, tm % 2

    def turned(dz, dy, flip=0):
        pairs = []
        for m in range(32):
            a, b, c = m // 8, (m // 2) % 4, m % 2
            pairs.append((m, ((a + dz) % 4) * 8 + ((b + dy) % 4) * 2 + (c + flip) % 2))
        return pairs

    def send(x, dz, dy, flip=0):
        return lax.ppermute(x, "tm", turned(dz, dy, flip))

    dilated = lax.all_gather(dilated_w, "tm", axis=1, tiled=True)
    up_t = jnp.transpose(upsample_w, (0, 2, 1))
    up_other = send(up_t, 0, 0, 1)
    up = jnp.where(
        core == 0,
        jnp.concatenate([up_t, up_other], axis=1),
        jnp.concatenate([up_other, up_t], axis=1),
    ).reshape(-1, up_t.shape[2])

    flat = jnp.transpose(cache_prev, (2, 0, 1)).reshape(slab, groups * past)
    cached = lax.all_to_all(
        jnp.broadcast_to(flat[None], (32,) + flat.shape), "tm", 0, 0, tiled=True
    ).reshape(32 * slab, groups * past)
    pad = 128 - width
    alpha_c = jnp.pad(alpha_coarse, (0, pad), constant_values=1.0)[None]
    inverse_c = 1.0 / alpha_c
    order = jnp.stack([core, 1 - core]).astype(jnp.int32)
    main, first = pl.pallas_call(
        coarse_kernel,
        grid_spec=pltpu.PrefetchScalarGridSpec(
            num_scalar_prefetch=1,
            grid=(2,),
            in_specs=[
                pl.BlockSpec((half, frames, depth), lambda i, o: (o[i], 0, 0)),
                whole(taps, depth, width),
                whole(1, 128),
                whole(1, 128),
            ],
            out_specs=[
                pl.BlockSpec((1, width, half * frames), lambda i, o: (i, 0, 0)),
                pl.BlockSpec((half * past, 128), lambda i, o: (o[i], 0)),
            ],
            scratch_shapes=[
                pltpu.VMEM((depth, 512), BF16),
                pltpu.VMEM((half * frames, 128), F32),
            ],
        ),
        out_shape=[
            jax.ShapeDtypeStruct((2, width, half * frames), BF16),
            jax.ShapeDtypeStruct((groups * past, 128), F32),
        ],
        compiler_params=pltpu.CompilerParams(vmem_limit_bytes=VMEM_LIMIT),
        name="coarse_main",
    )(order, latents, conv_in_w, alpha_c, inverse_c)
    own = jnp.concatenate([main[0], send(main[1], 0, 0, 1)], axis=0)
    cached = after(cached, own)
    added = pl.pallas_call(
        cached_kernel,
        grid=(1,),
        in_specs=[whole(depth, groups * past), whole(taps, depth, width)],
        out_specs=whole(groups * past // 2, 128),
        out_shape=jax.ShapeDtypeStruct((groups * past // 2, 128), BF16),
        scratch_shapes=[pltpu.VMEM((depth, 512), BF16), pltpu.VMEM((groups * past, 128), F32)],
        compiler_params=pltpu.CompilerParams(vmem_limit_bytes=VMEM_LIMIT),
        name="cached",
    )(cached, conv_in_w)
    every = lax.all_to_all(
        jnp.broadcast_to(added[None], (8,) + added.shape), "stream", 0, 0, tiled=True
    ).reshape(4 * groups * past, 128)
    low = jnp.concatenate([own, send(own, 1, 0)], axis=0)
    high = jnp.concatenate([send(own, 2, 0), send(own, 3, 0)], axis=0)
    up_low, down_low = send(low, 0, 1), send(low, 0, 3)
    up_high, down_high = send(high, 0, 1), send(high, 0, 3)
    far_low, far_high = send(up_low, 0, 1), send(down_high, 0, 3)
    columns = [low, high, up_low, up_high, far_low, far_high, down_low, down_high]

    head = pl.pallas_call(
        history_kernel,
        grid_spec=pltpu.PrefetchScalarGridSpec(
            num_scalar_prefetch=1,
            grid=(1,),
            in_specs=[
                whole(4 * groups * past, 128),
                whole(groups * past, 128),
                whole(1, 128),
                whole(1, 128),
            ],
            out_specs=whole(2, width, 128),
            scratch_shapes=[
                pltpu.VMEM((groups * past, 128), F32),
                pltpu.VMEM((4 * groups * past, 128), F32),
            ],
        ),
        out_shape=jax.ShapeDtypeStruct((2, width, 128), BF16),
        compiler_params=pltpu.CompilerParams(vmem_limit_bytes=VMEM_LIMIT),
        name="coarse_history",
    )(prev_slot, every, first, alpha_c, inverse_c)
    heads = lax.all_to_all(
        jnp.tile(head, (16, 1, 1)), "tm", 0, 0, tiled=True
    ).reshape(32 * width, 128)

    offsets = []
    for dy in range(4):
        for dz in range(4):
            for flip in range(2):
                source = ((z - dz) % 4) * 8 + ((y - dy) % 4) * 2 + (core + flip) % 2
                offsets.append(source * width)
    offsets = jnp.stack(offsets).astype(jnp.int32)
    n = half * frames
    blocks = pl.pallas_call(
        upsample_kernel,
        grid_spec=pltpu.PrefetchScalarGridSpec(
            num_scalar_prefetch=1,
            grid=(1,),
            in_specs=[whole(4 * width, n)] * 8
            + [whole(32 * width, 128), whole(16 * width, 32 * width)],
            out_specs=whole(32, 24, 8 * width),
            scratch_shapes=[
                pltpu.VMEM((32 * width, n), BF16),
                pltpu.VMEM((n + 8, 8 * width), F32),
            ],
        ),
        out_shape=jax.ShapeDtypeStruct((32, 24, 8 * width), BF16),
        compiler_params=pltpu.CompilerParams(vmem_limit_bytes=60 * 1024 * 1024),
        name="upsample",
    )(offsets, *columns, heads, up)
    arrived = lax.all_to_all(blocks, "tm", 0, 0, tiled=True)

    shard = 16
    rows = shard * groups
    limit = 8 * lengths - tm * shard
    limit = jnp.tile(limit, shard)[:, None].astype(jnp.int32)
    return pl.pallas_call(
        residual_kernel,
        grid=(1,),
        in_specs=[
            whole(32, 24, 8 * width),
            whole(rows, 1),
            whole(1, channels),
            whole(1, channels),
            whole(1, channels),
            whole(1, channels),
            pl.BlockSpec(memory_space=pl.ANY),
            whole(channels, channels),
        ],
        out_specs=whole(groups, shard, channels),
        out_shape=jax.ShapeDtypeStruct((groups, shard, channels), BF16),
        scratch_shapes=[
            pltpu.VMEM((24 * groups, channels), F32),
            pltpu.VMEM((24 * groups, channels), BF16),
            pltpu.VMEM((channels // 128, rows, 128), F32),
            pltpu.VMEM((taps, channels, channels), BF16),
            pltpu.SemaphoreType.DMA((taps,)),
        ],
        compiler_params=pltpu.CompilerParams(vmem_limit_bytes=VMEM_LIMIT),
        name="residual",
    )(
        arrived,
        limit,
        alpha_in[None],
        (1.0 / alpha_in)[None],
        alpha_mid[None],
        (1.0 / alpha_mid)[None],
        dilated,
        project_w,
    )


def solution(mesh):
    return jax.shard_map(
        per_device,
        mesh=mesh,
        in_specs=(
            P("stream", None, None),
            P("stream", None, "tm"),
            P("stream"),
            P("stream"),
            P(None, None, "tm"),
            P(None, None, "tm"),
            P("tm"),
            P(),
            P(),
            P(None, "tm", None),
            P(),
        ),
        out_specs=P("stream", "tm", None),
        check_vma=False,
    )
```

```python
import functools

import jax
import jax.numpy as jnp
from jax import lax
from jax.experimental import pallas as pl
from jax.experimental.pallas import tpu as pltpu
from jax.sharding import PartitionSpec as P

F32 = jnp.float32
BF16 = jnp.bfloat16
VMEM_LIMIT = 48 * 1024 * 1024


def sin_squared(u):
    k = jnp.floor(u * 0.3183098861837907 + 0.5)
    r = u - k * 3.140625
    r = r - k * 0.0009670257568359375
    r = r - k * 6.2771141529083252e-07
    r = jnp.clip(r, -1.5708, 1.5708)
    q = r * r
    p = -2.5052108385441720e-08
    p = p * q + 2.7557319223985893e-06
    p = p * q - 1.9841269841269841e-04
    p = p * q + 8.3333333333333333e-03
    p = p * q - 1.6666666666666667e-01
    s = r + r * (q * p)
    return s * s


def snake(x, alpha, inverse):
    return x + sin_squared(alpha * x) * inverse


def fill_taps(w_ref, wc_ref):
    taps, _, width = w_ref.shape
    wc_ref[...] = jnp.zeros_like(wc_ref)
    for k in range(taps):
        at = 64 * k
        wc_ref[:, at : at + width] = w_ref[k]


def tap_sum(y, shift, width):
    rows = y.shape[0]
    total = None
    for g in range(y.shape[1] // 128):
        part = y[:, 128 * g : 128 * g + 128]
        turn = (-(2 * g + shift)) % rows
        if turn:
            part = pltpu.roll(part, turn, 0)
        total = part if total is None else total + part
    odd = pltpu.roll(pltpu.roll(total, rows - 1, 0), 64, 1)
    return total + odd


def coarse_kernel(
    order_ref, lat_ref, w_ref, a_ref, ia_ref, out_ref, first_ref, wc_ref, v_ref
):
    half, frames, depth = lat_ref.shape
    width = out_ref.shape[1]

    @pl.when(pl.program_id(0) == 0)
    def _():
        fill_taps(w_ref, wc_ref)

    x = lat_ref[...].reshape(half * frames, depth)
    y = jnp.dot(x, wc_ref[...], preferred_element_type=F32)
    past = first_ref.shape[0] // half
    blank = jnp.zeros((past, y.shape[1]), F32)
    for s in range(half):
        ys = y[s * frames : (s + 1) * frames]
        v_ref[s * frames : (s + 1) * frames, :] = tap_sum(ys, -6, width)
        first_ref[past * s : past * (s + 1), :] = tap_sum(
            jnp.concatenate([blank, ys[:past]], axis=0), 0, width
        )[:past]
    u = [v_ref[pl.ds(t, half, stride=frames), :] for t in range(frames)]
    u = jnp.concatenate(u, axis=0)
    u = snake(u, a_ref[...], ia_ref[...])
    out_ref[0] = u.T[:width].astype(BF16)


def cached_kernel(h_ref, w_ref, out_ref, wc_ref, v_ref):
    fill_taps(w_ref, wc_ref)
    rows = h_ref.shape[1]
    past = 8
    ht = h_ref[...].astype(F32).T.astype(BF16)
    y = jnp.dot(ht, wc_ref[...], preferred_element_type=F32)
    blank = jnp.zeros((past, y.shape[1]), F32)
    for s in range(rows // past):
        z = jnp.concatenate([y[past * s : past * (s + 1)], blank], axis=0)
        v_ref[past * s : past * (s + 1), :] = tap_sum(z, 0, 48)[:past]
    packed = out_ref.shape[0]
    lane = lax.broadcasted_iota(jnp.int32, (packed, 128), 1)
    upper = pltpu.roll(v_ref[packed:, :], 64, 1)
    out_ref[...] = jnp.where(lane < 64, v_ref[:packed, :], upper).astype(BF16)


def history_kernel(
    slot_ref, c_ref, first_ref, a_ref, ia_ref, out_ref, v_ref, all_ref
):
    width = out_ref.shape[1]
    past = 8
    streams = first_ref.shape[0] // past
    half = streams // 2
    all_ref[...] = c_ref[...].astype(F32)
    for s in range(streams):
        slot = slot_ref[s]
        at = pl.multiple_of(((slot >> 4) * 8 + (slot & 7)) * past, past)
        cached = all_ref[pl.ds(at, past), :]
        upper = ((slot >> 3) & 1) * jnp.ones((past, 128), jnp.int32)
        cached = jnp.where(upper == 1, pltpu.roll(cached, 64, 1), cached)
        mine = slice(past * s, past * (s + 1))
        v_ref[mine, :] = first_ref[mine, :] + cached
    for c in range(2):
        rows = [
            v_ref[pl.ds(c * half * past + i, half, stride=past), :] for i in range(past)
        ]
        u = jnp.concatenate(rows[2:] + rows[:2], axis=0)
        u = snake(u, a_ref[...], ia_ref[...])
        u = jnp.concatenate([u, pltpu.roll(u, 128 - width, 1)], axis=0)
        out_ref[c] = u.T[:width].astype(BF16)


def upsample_kernel(off_ref, *refs):
    x_refs, (h_ref, w_ref, out_ref, xs_ref, fs_ref, xh_ref) = refs[:8], refs[8:]
    width = 48
    n = xs_ref.shape[1]
    pieces = x_refs[0].shape[0] // width
    for part, ref in enumerate(x_refs):
        for i in range(pieces):
            at = pl.multiple_of(off_ref[part * pieces + i], 16)
            xs_ref[pl.ds(at, width), :] = ref[i * width : (i + 1) * width, :]
    part = h_ref.shape[1]
    lane = lax.broadcasted_iota(jnp.int32, (part, 128), 1)
    for m in range(h_ref.shape[0]):
        h = h_ref[m].astype(F32)
        turned = pltpu.roll(h, 64, 1)
        both = [jnp.where(lane < 64, h, turned), jnp.where(lane < 64, turned, h)]
        xh_ref[m * width : (m + 1) * width, :] = jnp.concatenate(both, 0).astype(BF16)
    rows = w_ref.shape[0]
    half = rows // 2
    r = jnp.dot(w_ref[...], xs_ref[...], preferred_element_type=F32)
    rh = jnp.dot(w_ref[...], xh_ref[...], preferred_element_type=F32)
    lane = lax.broadcasted_iota(jnp.int32, (rows, 128), 1)
    first = jnp.where(lane < 48, rh, r[:, :128])
    r = jnp.concatenate([first, r[:, 128:]], axis=1)
    turned = pltpu.roll(rh[half:], 8, 1)
    shifted = pltpu.roll(r[half:], 8, 1)
    lane = lax.broadcasted_iota(jnp.int32, (half, 128), 1)
    shifted = jnp.concatenate(
        [jnp.where(lane < 8, turned, shifted[:, :128]), shifted[:, 128:]], axis=1
    )
    fs_ref[8 : 8 + n, :] = (r[:half] + shifted).T
    fs_ref[0:8, :] = (rh[:half] + turned).T[120:128]
    blocks, take, _ = out_ref.shape
    for b in range(blocks):
        out_ref[b] = fs_ref[16 * b : 16 * b + take, :].astype(BF16)


def residual_kernel(
    arr_ref, lim_ref, ai_ref, iai_ref, am_ref, iam_ref, wd_hbm, wp_ref,
    out_ref, f_ref, win_ref, r_ref, wd_ref, sems,
):
    streams, shard, channels = out_ref.shape
    rows = streams * shard
    sources, take, _ = arr_ref.shape
    taps = wd_ref.shape[0]
    piece = 48
    half = streams // 2
    copies = [
        pltpu.make_async_copy(wd_hbm.at[k], wd_ref.at[k], sems.at[k])
        for k in range(taps)
    ]
    for copy in copies:
        copy.start()
    for c in range(2):
        for j in range(8):
            x = jnp.concatenate(
                [
                    arr_ref[m, :, piece * j : piece * (j + 1)].astype(F32)
                    for m in range(c, sources, 2)
                ],
                axis=1,
            )
            for t in range(take // half):
                at = (8 * t + j) * streams + half * c
                f_ref[at : at + half, :] = x[half * t : half * (t + 1)]
    used = 2 * streams
    win_ref[used:, :] = snake(f_ref[used:, :], ai_ref[...], iai_ref[...]).astype(BF16)
    total = None
    for k in range(taps):
        copies[k].wait()
        at = (k + 2) * streams
        part = jnp.dot(
            win_ref[at : at + rows, :], wd_ref[k], preferred_element_type=F32
        )
        total = part if total is None else total + part
    middle = snake(total, am_ref[...], iam_ref[...]).astype(BF16)
    summed = f_ref[8 * streams :, :] + jnp.dot(
        middle, wp_ref[...], preferred_element_type=F32
    )
    local = lax.broadcasted_iota(jnp.int32, (rows, channels), 0) // streams
    kept = jnp.where(local < lim_ref[...], summed, 0.0)
    for g in range(channels // 128):
        r_ref[g] = kept[:, 128 * g : 128 * (g + 1)]
    for s in range(streams):
        out_ref[s] = jnp.concatenate(
            [
                r_ref[g, pl.ds(s, shard, stride=streams), :]
                for g in range(channels // 128)
            ],
            axis=1,
        ).astype(BF16)


def after(x, *others):
    return lax.optimization_barrier((x,) + others)[0]


def whole(*shape):
    return pl.BlockSpec(shape, lambda *_: (0,) * len(shape))


def per_device(
    latents,
    cache_prev,
    prev_slot,
    lengths,
    conv_in_w,
    upsample_w,
    alpha_coarse,
    alpha_in,
    alpha_mid,
    dilated_w,
    project_w,
):
    groups, frames, depth = latents.shape
    taps, _, width = conv_in_w.shape
    past = cache_prev.shape[1]
    slab = cache_prev.shape[2]
    half = groups // 2
    channels = dilated_w.shape[2]
    tm = lax.axis_index("tm")
    z, y, core = tm // 8, (tm // 2) % 4, tm % 2

    def turned(dz, dy, flip=0):
        pairs = []
        for m in range(32):
            a, b, c = m // 8, (m // 2) % 4, m % 2
            pairs.append((m, ((a + dz) % 4) * 8 + ((b + dy) % 4) * 2 + (c + flip) % 2))
        return pairs

    def send(x, dz, dy, flip=0):
        return lax.ppermute(x, "tm", turned(dz, dy, flip))

    dilated = lax.all_gather(dilated_w, "tm", axis=1, tiled=True)
    up_t = jnp.transpose(upsample_w, (0, 2, 1))
    up_other = send(up_t, 0, 0, 1)
    up = jnp.where(
        core == 0,
        jnp.concatenate([up_t, up_other], axis=1),
        jnp.concatenate([up_other, up_t], axis=1),
    ).reshape(-1, up_t.shape[2])

    flat = jnp.transpose(cache_prev, (2, 0, 1)).reshape(slab, groups * past)
    cached = lax.all_to_all(
        jnp.broadcast_to(flat[None], (32,) + flat.shape), "tm", 0, 0, tiled=True
    ).reshape(32 * slab, groups * past)
    pad = 128 - width
    alpha_c = jnp.pad(alpha_coarse, (0, pad), constant_values=1.0)[None]
    inverse_c = 1.0 / alpha_c
    order = jnp.stack([core, 1 - core]).astype(jnp.int32)
    main, first = pl.pallas_call(
        coarse_kernel,
        grid_spec=pltpu.PrefetchScalarGridSpec(
            num_scalar_prefetch=1,
            grid=(2,),
            in_specs=[
                pl.BlockSpec((half, frames, depth), lambda i, o: (o[i], 0, 0)),
                whole(taps, depth, width),
                whole(1, 128),
                whole(1, 128),
            ],
            out_specs=[
                pl.BlockSpec((1, width, half * frames), lambda i, o: (i, 0, 0)),
                pl.BlockSpec((half * past, 128), lambda i, o: (o[i], 0)),
            ],
            scratch_shapes=[
                pltpu.VMEM((depth, 512), BF16),
                pltpu.VMEM((half * frames, 128), F32),
            ],
        ),
        out_shape=[
            jax.ShapeDtypeStruct((2, width, half * frames), BF16),
            jax.ShapeDtypeStruct((groups * past, 128), F32),
        ],
        compiler_params=pltpu.CompilerParams(vmem_limit_bytes=VMEM_LIMIT),
        name="coarse_main",
    )(order, latents, conv_in_w, alpha_c, inverse_c)
    own = jnp.concatenate([main[0], send(main[1], 0, 0, 1)], axis=0)
    cached = after(cached, own)
    added = pl.pallas_call(
        cached_kernel,
        grid=(1,),
        in_specs=[whole(depth, groups * past), whole(taps, depth, width)],
        out_specs=whole(groups * past // 2, 128),
        out_shape=jax.ShapeDtypeStruct((groups * past // 2, 128), BF16),
        scratch_shapes=[pltpu.VMEM((depth, 512), BF16), pltpu.VMEM((groups * past, 128), F32)],
        compiler_params=pltpu.CompilerParams(vmem_limit_bytes=VMEM_LIMIT),
        name="cached",
    )(cached, conv_in_w)
    every = lax.all_to_all(
        jnp.broadcast_to(added[None], (8,) + added.shape), "stream", 0, 0, tiled=True
    ).reshape(4 * groups * past, 128)
    low = jnp.concatenate([own, send(own, 1, 0)], axis=0)
    high = jnp.concatenate([send(own, 2, 0), send(own, 3, 0)], axis=0)
    up_low, down_low = send(low, 0, 1), send(low, 0, 3)
    up_high, down_high = send(high, 0, 1), send(high, 0, 3)
    far_low, far_high = send(up_low, 0, 1), send(down_high, 0, 3)
    columns = [low, high, up_low, up_high, far_low, far_high, down_low, down_high]

    head = pl.pallas_call(
        history_kernel,
        grid_spec=pltpu.PrefetchScalarGridSpec(
            num_scalar_prefetch=1,
            grid=(1,),
            in_specs=[
                whole(4 * groups * past, 128),
                whole(groups * past, 128),
                whole(1, 128),
                whole(1, 128),
            ],
            out_specs=whole(2, width // 2, 128),
            scratch_shapes=[
                pltpu.VMEM((groups * past, 128), F32),
                pltpu.VMEM((4 * groups * past, 128), F32),
            ],
        ),
        out_shape=jax.ShapeDtypeStruct((2, width // 2, 128), BF16),
        compiler_params=pltpu.CompilerParams(vmem_limit_bytes=VMEM_LIMIT),
        name="coarse_history",
    )(prev_slot, every, first, alpha_c, inverse_c)
    heads = lax.all_to_all(
        jnp.tile(head, (16, 1, 1)), "tm", 0, 0, tiled=True
    ).reshape(32, width // 2, 128)

    offsets = []
    for dy in range(4):
        for dz in range(4):
            for flip in range(2):
                source = ((z - dz) % 4) * 8 + ((y - dy) % 4) * 2 + (core + flip) % 2
                offsets.append(source * width)
    offsets = jnp.stack(offsets).astype(jnp.int32)
    n = half * frames
    blocks = pl.pallas_call(
        upsample_kernel,
        grid_spec=pltpu.PrefetchScalarGridSpec(
            num_scalar_prefetch=1,
            grid=(1,),
            in_specs=[whole(4 * width, n)] * 8
            + [whole(32, width // 2, 128), whole(16 * width, 32 * width)],
            out_specs=whole(32, 24, 8 * width),
            scratch_shapes=[
                pltpu.VMEM((32 * width, n), BF16),
                pltpu.VMEM((n + 8, 8 * width), F32),
                pltpu.VMEM((32 * width, 128), BF16),
            ],
        ),
        out_shape=jax.ShapeDtypeStruct((32, 24, 8 * width), BF16),
        compiler_params=pltpu.CompilerParams(vmem_limit_bytes=60 * 1024 * 1024),
        name="upsample",
    )(offsets, *columns, heads, up)
    arrived = lax.all_to_all(blocks, "tm", 0, 0, tiled=True)

    shard = 16
    rows = shard * groups
    limit = 8 * lengths - tm * shard
    limit = jnp.tile(limit, shard)[:, None].astype(jnp.int32)
    return pl.pallas_call(
        residual_kernel,
        grid=(1,),
        in_specs=[
            whole(32, 24, 8 * width),
            whole(rows, 1),
            whole(1, channels),
            whole(1, channels),
            whole(1, channels),
            whole(1, channels),
            pl.BlockSpec(memory_space=pl.ANY),
            whole(channels, channels),
        ],
        out_specs=whole(groups, shard, channels),
        out_shape=jax.ShapeDtypeStruct((groups, shard, channels), BF16),
        scratch_shapes=[
            pltpu.VMEM((24 * groups, channels), F32),
            pltpu.VMEM((24 * groups, channels), BF16),
            pltpu.VMEM((channels // 128, rows, 128), F32),
            pltpu.VMEM((taps, channels, channels), BF16),
            pltpu.SemaphoreType.DMA((taps,)),
        ],
        compiler_params=pltpu.CompilerParams(vmem_limit_bytes=VMEM_LIMIT),
        name="residual",
    )(
        arrived,
        limit,
        alpha_in[None],
        (1.0 / alpha_in)[None],
        alpha_mid[None],
        (1.0 / alpha_mid)[None],
        dilated,
        project_w,
    )


def solution(mesh):
    return jax.shard_map(
        per_device,
        mesh=mesh,
        in_specs=(
            P("stream", None, None),
            P("stream", None, "tm"),
            P("stream"),
            P("stream"),
            P(None, None, "tm"),
            P(None, None, "tm"),
            P("tm"),
            P(),
            P(),
            P(None, "tm", None),
            P(),
        ),
        out_specs=P("stream", "tm", None),
        check_vma=False,
    )
```
